512 devices in a mesh: dp: 64 (over z, y_hi, core), replica: 8 (over y_lo, x).
Axes of the slice: x: 4, y: 4 (y_hi: 2, y_lo: 2; y = y_hi * 2 + y_lo), z: 16, core: 2. Of those that a mesh axis runs over, the one named last changes fastest.
Arguments:
- img_emb: bfloat16 [8, 8192, 768], P('replica', 'dp')
- txt_base: bfloat16 [8, 8192, 768], P('replica', 'dp')
- txt_feat: bfloat16 [8, 8192, 640], P('replica', 'dp'), may hold values from -6 to 6
- head: float32 [640, 768], P('dp'), may hold values from -0.25 to 0.25
- momentum: float32 [640, 768], P('dp'), may hold values from -3 to 3
- positive_image: int32 [8, 8192], P('replica', 'dp'), may hold values from 0 to 8191, each once within a row
Outputs:
- new_head: float32 [640, 768], P('dp')
- new_momentum: float32 [640, 768], P('dp')
The draws below stay inside these ranges and needn't reach their ends.
Inputs may be any that keep to these rules, and one draw needn't show every extreme that they name: `positive_image`: in each replica the 8192 texts name 8192 different images.
All inputs are finite; a program needn't handle non-finite values.
Results may differ from the reference program's by a relative error of at most 0.005.
Values may be sent and summed in bfloat16 or wider, within the bound.
A program may use at most 64 MiB of HBM per device.

```python
import jax
import jax.numpy as jnp
from jax import lax

D = 768
K = 640
PAIRS_DEV = 128
PAIRS = 8192
REPLICAS = 8
N_DP = 64


def draw_img_emb(key, part):
    key = jax.random.fold_in(key, 11)
    return jax.random.normal(key, (REPLICAS, PAIRS, D), jnp.float32).astype(jnp.bfloat16)


def draw_txt_base(key, part):
    key = jax.random.fold_in(key, 12)
    return jax.random.normal(key, (REPLICAS, PAIRS, D), jnp.float32).astype(jnp.bfloat16)


def shard_levels(rng, dims, shards, low, largest):
    loudness = 1.0
    for position, blocks in shards:
        draws = jax.random.uniform(jax.random.fold_in(jax.random.fold_in(rng, 6), position), (blocks,), jnp.float32, low / len(shards), largest / len(shards))
        loudness = loudness * jnp.repeat(jnp.exp(draws), dims[position] // blocks).reshape((-1,) + (1,) * (len(dims) - 1 - position))
    return loudness


def centred(stream_key, dims, deviation, bound, shards=(), kind=jnp.bfloat16):
    result = deviation * jax.random.normal(stream_key, dims, jnp.float32)
    if shards:
        result = result * shard_levels(stream_key, dims, shards, -0.22, 0.18)
    return jnp.clip(result, -bound, bound).astype(kind)


def setup_inputs(seed: int = 0) -> dict:
    splits = jax.random.split(jax.random.key(seed), 7)
    img_emb = draw_img_emb(jax.random.fold_in(splits[6], 71), 0)
    txt_base = draw_txt_base(jax.random.fold_in(splits[6], 71), 0)
    txt_feat = centred(splits[2], (REPLICAS, PAIRS, K), 1.0, 6.0, ((0, 8), (1, 64)))
    head = centred(splits[3], (K, D), K ** -0.5, 0.25, ((0, 64),), jnp.float32)
    momentum = centred(splits[4], (K, D), 0.5, 3.0, ((0, 64),), jnp.float32)
    positive_image = jax.vmap(lambda own: jax.random.permutation(own, PAIRS))(jax.random.split(splits[5], REPLICAS)).reshape((REPLICAS, PAIRS)).astype(jnp.int32)
    return dict(img_emb=img_emb, txt_base=txt_base, txt_feat=txt_feat, head=head, momentum=momentum, positive_image=positive_image)


logit_scale = 10.0
logit_bias = -3.0
norm_epsilon = 1e-06
momentum_decay = 0.9
blend_weight = 0.7
outer_rate = 0.7

def reference(img_emb, txt_base, txt_feat, head, momentum, positive_image):
    head_low = head.astype(jnp.bfloat16)

    def one_replica(inputs):
        images, base, features, labels = inputs
        image_wide = images.astype(jnp.float32)
        image_unit = (image_wide * lax.rsqrt(lax.optimization_barrier(jnp.sum(image_wide * image_wide, axis=1, keepdims=True)) + norm_epsilon)).astype(jnp.bfloat16)
        text_emb = base.astype(jnp.float32) + jnp.dot(features, head_low, preferred_element_type=jnp.float32)
        inv_norm = lax.rsqrt(lax.optimization_barrier(jnp.sum(text_emb * text_emb, axis=1, keepdims=True)) + norm_epsilon)
        text_exact = text_emb * inv_norm
        text_unit = text_exact.astype(jnp.bfloat16)
        blocks = (text_unit.reshape(N_DP, PAIRS_DEV, D), labels.reshape(N_DP, PAIRS_DEV))
        columns = jnp.arange(PAIRS, dtype=jnp.int32)

        def block_grad(item):
            rows, targets = item
            logits = logit_scale * lax.dot_general(rows, image_unit, (((1,), (1,)), ((), ())), preferred_element_type=jnp.float32) + logit_bias
            matches = (targets[:, None] == columns[None, :]).astype(jnp.float32)
            weights = (jax.nn.sigmoid(logits) - matches).astype(jnp.bfloat16)
            return jnp.dot(weights, image_unit, preferred_element_type=jnp.float32)
        unit_grad = logit_scale * lax.map(block_grad, blocks).reshape(PAIRS, D)
        along = lax.optimization_barrier(jnp.sum(text_exact * unit_grad, axis=1, keepdims=True))
        text_grad = ((unit_grad - text_exact * along) * inv_norm).astype(jnp.bfloat16)
        return lax.dot_general(features, text_grad, (((0,), (0,)), ((), ())), preferred_element_type=jnp.float32)
    grads = lax.map(one_replica, (img_emb, txt_base, txt_feat, positive_image))
    head_grad = lax.optimization_barrier(jnp.sum(grads, axis=0)) / REPLICAS
    new_momentum = momentum_decay * momentum + (1.0 - momentum_decay) * head_grad
    new_head = head - outer_rate * ((1.0 - blend_weight) * head_grad + blend_weight * new_momentum)
    return (new_head, new_momentum)
```

```python
import functools

import jax
import jax.numpy as jnp
from jax import lax
from jax.experimental import pallas as pl
from jax.experimental.pallas import tpu as pltpu
from jax.sharding import PartitionSpec as P

MESH = pl.DeviceIdType.MESH
F32 = jnp.float32
BF16 = jnp.bfloat16

logit_scale = 10.0
logit_bias = -3.0
norm_epsilon = 1e-06
momentum_decay = 0.9
blend_weight = 0.7
outer_rate = 0.7

NZ = 16
ROWS = 128
D = 768
K = 640
OWN = 10
PAD = 16
HALF = D // 2
NT = (((1,), (1,)), ((), ()))
CHUNKS = 4
PIECE = ROWS // CHUNKS


def kernel(
    img_hbm,
    base_hbm,
    feat_hbm,
    head_ref,
    momentum_ref,
    label_hbm,
    new_head_ref,
    new_momentum_ref,
    img_raw,
    img,
    tb,
    tf,
    tl,
    hb,
    pick,
    order,
    spread,
    feat_t,
    text_exact,
    text_unit,
    inv_norm,
    label_wide,
    unit_grad,
    grad_low,
    core_out,
    core_in,
    x_own,
    x_out,
    x_in,
    y_out,
    y_in,
    z_out,
    z_in,
    share,
    local_sem,
    up_send,
    up_recv,
    dn_send,
    dn_recv,
    text_send,
    text_recv,
    hz_send,
    hz_recv,
    hy_send,
    hy_recv,
    hx_send,
    hx_recv,
    hc_send,
    hc_recv,
    gc_send,
    gc_recv,
    gx_send,
    gx_recv,
    gy_send,
    gy_recv,
    gz_send,
    gz_recv,
    gb_send,
    gb_recv,
):
    dp = lax.axis_index("dp")
    rep = lax.axis_index("replica")
    z, yh, c = dp // 4, (dp // 2) % 2, dp % 2
    yl, x = rep // 4, rep % 4
    y = yl + 2 * yh

    def at(z2, y2, x2, c2):
        return (z2 * 4 + (y2 // 2) * 2 + c2, (y2 % 2) * 4 + x2)

    def to_z(k):
        return at((z + k) % NZ, y, x, c)

    def to_y(k):
        return at(z, (y + k) % 4, x, c)

    def to_x(k):
        return at(z, y, (x + k) % 4, c)

    to_core = at(z, y, x, 1 - c)

    def remote(src, dst, send, recv, device):
        return pltpu.make_async_remote_copy(
            src_ref=src, dst_ref=dst, send_sem=send, recv_sem=recv, device_id=device, device_id_type=MESH
        )

    loads = [
        pltpu.make_async_copy(img_hbm, img_raw, local_sem.at[0]),
        pltpu.make_async_copy(base_hbm, tb.at[0], local_sem.at[1]),
        pltpu.make_async_copy(feat_hbm, tf.at[0], local_sem.at[2]),
        pltpu.make_async_copy(label_hbm, tl.at[0], local_sem.at[3]),
    ]
    for load in loads:
        load.start()

    barrier = pltpu.get_barrier_semaphore()

    def greet(device):
        pl.semaphore_signal(barrier, inc=1, device_id=device, device_id_type=MESH)

    def greet_z(k, carry):
        greet(to_z(k))
        return carry

    lax.fori_loop(1, NZ, greet_z, 0)
    greet(to_core)
    for k in range(1, 4):
        greet(to_x(k))
        greet(to_y(k))
        greet(at(z, yh * 2 + (1 - yl), (x + k) % 4, c))

    loads[0].wait()
    wide = img_raw[...].astype(F32)
    img[0] = (wide * lax.rsqrt(jnp.sum(wide * wide, axis=1, keepdims=True) + norm_epsilon)).astype(BF16)

    def head_block(c2, x2, yl2, yh2, zh2):
        return (((c2 * 4 + x2) * 2 + yl2) * 2 + yh2) * 2 + zh2

    is_source = (z % 8) == rep
    own_block = head_block(c, x, yl, yh, z // 8)
    head_low = jnp.concatenate([head_ref[...], jnp.zeros((PAD - OWN, D), F32)], axis=0).astype(BF16)

    @pl.when(is_source)
    def _():
        hb[own_block] = head_low

    pl.semaphore_wait(barrier, 15 + 1 + 9)

    def head_z(k):
        block = hb.at[own_block]
        return remote(block, block, hz_send.at[k], hz_recv.at[z // 8], to_z(k))

    @pl.when(is_source)
    def _():
        def go(k, carry):
            head_z(k).start()
            return carry

        lax.fori_loop(1, NZ, go, 0)

    def text_copies(src, slot, device, first):
        return [
            remote(s, d, text_send.at[first + i], text_recv.at[first + i], device)
            for i, (s, d) in enumerate(zip(src, (tb.at[slot], tf.at[slot], tl.at[slot])))
        ]

    own_text = (base_hbm, feat_hbm, label_hbm)
    text_y = text_copies(own_text, 2, to_y(2), 0)
    text_c = text_copies(own_text, 1, to_core, 3)
    text_yc = text_copies((tb.at[2], tf.at[2], tl.at[2]), 3, to_core, 6)
    for copy in text_y:
        copy.start()

    def up(s, k):
        rows = pl.ds(k * PIECE, PIECE)
        src, dst = jnp.maximum(2 * s - 3, 0), 2 * s - 1
        return remote(img.at[src, rows], img.at[dst, rows], up_send.at[s, k], up_recv.at[s, k], to_z(1))

    def dn(s, k):
        rows = pl.ds(k * PIECE, PIECE)
        src, dst = 2 * s - 2, jnp.minimum(2 * s, 15)
        return remote(img.at[src, rows], img.at[dst, rows], dn_send.at[s, k], dn_recv.at[s, k], to_z(NZ - 1))

    for k in range(CHUNKS):
        up(1, k).start()
        dn(1, k).start()
    for copy in text_c:
        copy.start()

    def ring(s):
        for k in range(CHUNKS):
            up(s, k).wait_recv()

            @pl.when((s < 7) | (k < CHUNKS // 2))
            def _():
                up(s + 1, k).start()

            dn(s, k).wait_recv()

            @pl.when((s < 7) | (k >= CHUNKS // 2))
            def _():
                dn(s + 1, k).start()

    place = lax.broadcasted_iota(jnp.int32, (1, 64 * PAD), 1)
    block, row = place >> 4, place & 15
    source = ((block >> 3) & 3) + 4 * ((block >> 2) & 1) + 8 * (block & 1)
    wanted = (source * 4 + ((block >> 1) & 1) * 2 + (block >> 5)) * OWN + row
    wanted = jnp.where(row < OWN, wanted, -1)
    pick[...] = (lax.broadcasted_iota(jnp.int32, (K, 64 * PAD), 0) == wanted).astype(F32).astype(BF16)

    place = lax.broadcasted_iota(jnp.int32, (K, 1), 0)
    block = (place * 6554) >> 16
    row = place - block * OWN
    source = ((block >> 4) & 1) * 2 + ((block >> 2) & 1) + 4 * (block & 3)
    owner = source * 4 + ((block >> 3) & 1) * 2 + (c ^ 1 ^ (block >> 5))
    wanted = owner * OWN + row
    order[...] = (lax.broadcasted_iota(jnp.int32, (K, K), 1) == wanted).astype(F32).astype(BF16)

    for zh in range(2):

        @pl.when(z != rep + 8 * zh)
        def _():
            block = hb.at[head_block(c, x, yl, yh, zh)]
            remote(block, block, hz_send.at[0], hz_recv.at[zh], to_z(1)).wait_recv()

    def head_y(k):
        blocks = hb.at[pl.ds(head_block(c, x, yl, yh, 0), 2)]
        return remote(blocks, blocks, hy_send.at[k], hy_recv.at[k], to_y(k))

    def head_x(k):
        blocks = hb.at[pl.ds(head_block(c, x, 0, 0, 0), 8)]
        return remote(blocks, blocks, hx_send.at[k], hx_recv.at[k], to_x(k))

    all_mine = hb.at[pl.ds(c * 32, 32)]
    head_c = remote(all_mine, all_mine, hc_send, hc_recv, to_core)

    for k in range(1, 4):
        head_y(k).start()
    ring(1)
    for k in range(1, 4):
        head_y(k).wait_recv()
    for k in range(1, 4):
        head_x(k).start()
    ring(2)
    for copy in text_y:
        copy.wait_recv()
    for copy in text_yc:
        copy.start()
    for k in range(1, 4):
        head_x(k).wait_recv()
    head_c.start()
    ring(3)

    for load in loads[1:]:
        load.wait()
    for copy in text_c + text_yc:
        copy.wait_recv()
    features = tf[...].reshape(4 * ROWS, K)
    spread[...] = jnp.dot(features, pick[...], preferred_element_type=F32).astype(BF16)
    feat_t[...] = lax.dot_general(order[...], features, NT, preferred_element_type=F32).astype(BF16)
    diagonal = lax.broadcasted_iota(jnp.int32, (ROWS, ROWS), 0) == lax.broadcasted_iota(jnp.int32, (ROWS, ROWS), 1)
    for i in range(4):
        column = jnp.sum(jnp.where(diagonal, tl[i].astype(F32), 0.0), axis=1, keepdims=True)
        label_wide[pl.ds(i * ROWS, ROWS)] = jnp.broadcast_to(column, (ROWS, ROWS)).astype(jnp.int32)
    head_c.wait_recv()
    head_all = hb[...].reshape(64 * PAD, D)
    for i in range(4):
        rows = pl.ds(i * ROWS, ROWS)
        emb = tb[i].astype(F32) + jnp.dot(spread[rows], head_all, preferred_element_type=F32)
        inv = lax.rsqrt(jnp.sum(emb * emb, axis=1, keepdims=True) + norm_epsilon)
        exact = emb * inv
        inv_norm[rows] = inv
        text_exact[rows] = exact
        text_unit[rows] = exact.astype(BF16)

    lane = lax.broadcasted_iota(jnp.int32, (1, ROWS), 1)

    def columns(z2):
        return ((z2 % NZ) * 4 + yh * 2 + c) * ROWS + lane

    def process(images, marks, fresh):
        for i in range(2):
            rows = pl.ds(i * 256, 256)
            raw = lax.dot_general(text_unit[rows], images, NT, preferred_element_type=F32)
            chance = 0.5 * jnp.tanh((0.5 * logit_scale) * raw + 0.5 * logit_bias) + 0.5
            labels = label_wide[rows]
            match = jnp.concatenate([(labels == m) for m in marks], axis=1)
            weights = jnp.where(match, chance - 1.0, chance).astype(BF16)
            grad = jnp.dot(weights, images, preferred_element_type=F32)
            if fresh:
                unit_grad[rows] = grad
            else:
                unit_grad[rows] += grad

    process(img[0], [columns(z)], True)

    def pair(p, carry):
        @pl.when(p % 2 == 1)
        def _():
            ring(4 + p // 2)

        images = img[pl.ds(2 * p - 1, 2)].reshape(2 * ROWS, D)
        process(images, [columns(z - p + NZ), columns(z + p)], False)
        return carry

    lax.fori_loop(1, 8, pair, 0)
    for k in range(CHUNKS // 2):
        up(8, k).wait_recv()
        dn(8, k + CHUNKS // 2).wait_recv()
    process(img[15], [columns(z + 8)], False)

    for i in range(4):
        rows = pl.ds(i * ROWS, ROWS)
        exact, grad = text_exact[rows], unit_grad[rows]
        along = jnp.sum(exact * grad, axis=1, keepdims=True)
        grad_low[rows] = ((grad - exact * along) * (logit_scale * inv_norm[rows])).astype(BF16)

    def to_other(h):
        return remote(core_out.at[h], core_in.at[h], gc_send.at[h], gc_recv.at[h], to_core)

    for h in range(2):
        core_out[h] = jnp.dot(feat_t[pl.ds(h * 160, 160)], grad_low[...], preferred_element_type=F32).astype(BF16)
        to_other(h).start()
    for h in range(2):
        mine = jnp.dot(feat_t[pl.ds(320 + h * 160, 160)], grad_low[...], preferred_element_type=F32)
        to_other(h).wait_recv()
        mine += core_in[h].astype(F32)
        for side in range(2):
            part = mine[:, side * HALF : (side + 1) * HALF]
            x_own[2 * h + side] = part
            x_out[2 * h + side] = part.astype(BF16)

    def to_x_part(k):
        return remote(x_out.at[(x + k) % 4], x_in.at[k - 1], gx_send.at[k], gx_recv.at[k], to_x(k))

    for k in range(1, 4):
        to_x_part(k).start()
    total = x_own[x]
    for k in range(1, 4):
        to_x_part(k).wait_recv()
        total += x_in[k - 1].astype(F32)
    for k in range(4):
        y_out[k] = total[k * 40 : (k + 1) * 40]

    def to_y_part(k):
        return remote(y_out.at[(y + k) % 4], y_in.at[k - 1], gy_send.at[k], gy_recv.at[k], to_y(k))

    for k in range(1, 4):
        to_y_part(k).start()
    total = y_out[y]
    for k in range(1, 4):
        to_y_part(k).wait_recv()
        total += y_in[k - 1]
    for j in range(4):
        z_out[j] = jnp.concatenate([total[j * OWN : (j + 1) * OWN], jnp.zeros((PAD - OWN, HALF), F32)], axis=0)

    group = 2 * (x // 2) + yl

    def to_z_part(j):
        k = (group + 4 * j - z + NZ) % NZ
        return remote(z_out.at[j], z_in.at[k], gz_send.at[j], gz_recv.at[k], to_z(k))

    for j in range(4):

        @pl.when(z != group + 4 * j)
        def _():
            to_z_part(j).start()

    is_owner = (z % 4) == group
    side = x % 2

    def to_share(i):
        rep2 = (rep + i) % 8
        device = (dp, rep2)
        return remote(share.at[side], share.at[side], gb_send.at[i], gb_recv.at[side], device)

    @pl.when(is_owner)
    def _():
        z_in[0] = z_out[z // 4]
        for k in range(1, NZ):
            remote(z_out.at[0], z_in.at[k], gz_send.at[0], gz_recv.at[k], to_z(1)).wait_recv()
        share[side] = jnp.sum(z_in[...], axis=0)
        for i in range(1, 8):
            to_share(i).start()

    for s in range(2):

        @pl.when(jnp.logical_not(is_owner & (side == s)))
        def _():
            remote(share.at[s], share.at[s], gb_send.at[0], gb_recv.at[s], to_x(1)).wait_recv()

    head_grad = jnp.concatenate([share[0, :OWN], share[1, :OWN]], axis=1) * (1.0 / 8.0)
    momentum = momentum_decay * momentum_ref[...] + (1.0 - momentum_decay) * head_grad
    new_momentum_ref[...] = momentum
    new_head_ref[...] = head_ref[...] - outer_rate * ((1.0 - blend_weight) * head_grad + blend_weight * momentum)

    @pl.when(is_source)
    def _():
        def drain(k, carry):
            head_z(k).wait_send()
            return carry

        lax.fori_loop(1, NZ, drain, 0)

    for copy in text_y + text_c + text_yc + [head_c]:
        copy.wait_send()

    def drain_ring(s, carry):
        for k in range(CHUNKS):
            up(s, k).wait_send()
            dn(s, k).wait_send()
        return carry

    lax.fori_loop(1, 8, drain_ring, 0)
    for k in range(CHUNKS // 2):
        up(8, k).wait_send()
        dn(8, k + CHUNKS // 2).wait_send()
    for k in range(1, 4):
        head_y(k).wait_send()
        head_x(k).wait_send()
        to_x_part(k).wait_send()
        to_y_part(k).wait_send()
    for h in range(2):
        to_other(h).wait_send()
    for j in range(4):

        @pl.when(z != group + 4 * j)
        def _():
            to_z_part(j).wait_send()

    @pl.when(is_owner)
    def _():
        for i in range(1, 8):
            to_share(i).wait_send()


def per_device(img_emb, txt_base, txt_feat, head, momentum, positive_image):
    vmem = pl.BlockSpec(memory_space=pltpu.VMEM)
    hbm = pl.BlockSpec(memory_space=pl.ANY)
    dma = pltpu.SemaphoreType.DMA
    texts = 4 * ROWS
    out = jax.ShapeDtypeStruct((OWN, D), F32)
    return pl.pallas_call(
        kernel,
        out_shape=(out, out),
        in_specs=[hbm, hbm, hbm, vmem, vmem, hbm],
        out_specs=(vmem, vmem),
        scratch_shapes=[
            pltpu.VMEM((ROWS, D), BF16),
            pltpu.VMEM((NZ, ROWS, D), BF16),
            pltpu.VMEM((4, ROWS, D), BF16),
            pltpu.VMEM((4, ROWS, K), BF16),
            pltpu.VMEM((4, 1, ROWS), jnp.int32),
            pltpu.VMEM((64, PAD, D), BF16),
            pltpu.VMEM((K, 64 * PAD), BF16),
            pltpu.VMEM((K, K), BF16),
            pltpu.VMEM((texts, 64 * PAD), BF16),
            pltpu.VMEM((K, texts), BF16),
            pltpu.VMEM((texts, D), F32),
            pltpu.VMEM((texts, D), BF16),
            pltpu.VMEM((texts, 1), F32),
            pltpu.VMEM((texts, ROWS), jnp.int32),
            pltpu.VMEM((texts, D), F32),
            pltpu.VMEM((texts, D), BF16),
            pltpu.VMEM((2, 160, D), BF16),
            pltpu.VMEM((2, 160, D), BF16),
            pltpu.VMEM((4, 160, HALF), F32),
            pltpu.VMEM((4, 160, HALF), BF16),
            pltpu.VMEM((3, 160, HALF), BF16),
            pltpu.VMEM((4, 40, HALF), F32),
            pltpu.VMEM((3, 40, HALF), F32),
            pltpu.VMEM((4, PAD, HALF), F32),
            pltpu.VMEM((NZ, PAD, HALF), F32),
            pltpu.VMEM((2, PAD, HALF), F32),
            dma((4,)),
            dma((9, CHUNKS)),
            dma((9, CHUNKS)),
            dma((9, CHUNKS)),
            dma((9, CHUNKS)),
            dma((9,)),
            dma((9,)),
            dma((NZ,)),
            dma((2,)),
            dma((4,)),
            dma((4,)),
            dma((4,)),
            dma((4,)),
            dma,
            dma,
            dma((2,)),
            dma((2,)),
            dma((4,)),
            dma((4,)),
            dma((4,)),
            dma((4,)),
            dma((4,)),
            dma((NZ,)),
            dma((8,)),
            dma((2,)),
        ],
        compiler_params=pltpu.CompilerParams(
            collective_id=0, has_side_effects=True, vmem_limit_bytes=48 * 1024 * 1024
        ),
        cost_estimate=pl.CostEstimate(flops=8_000_000_000, bytes_accessed=2_000_000, transcendentals=1_100_000),
        name="contrastive_step",
    )(img_emb[0], txt_base[0], txt_feat[0], head, momentum, positive_image)


def solution(mesh):
    placed = (
        P("replica", "dp", None),
        P("replica", "dp", None),
        P("replica", "dp", None),
        P("dp", None),
        P("dp", None),
        P("replica", "dp"),
    )
    return jax.shard_map(
        per_device,
        mesh=mesh,
        in_specs=placed,
        out_specs=(P("dp", None), P("dp", None)),
        check_vma=False,
    )
```

```python
import functools

import jax
import jax.numpy as jnp
from jax import lax
from jax.experimental import pallas as pl
from jax.experimental.pallas import tpu as pltpu
from jax.sharding import PartitionSpec as P

MESH = pl.DeviceIdType.MESH
F32 = jnp.float32
BF16 = jnp.bfloat16

logit_scale = 10.0
logit_bias = -3.0
norm_epsilon = 1e-06
momentum_decay = 0.9
blend_weight = 0.7
outer_rate = 0.7

NZ = 16
ROWS = 128
D = 768
K = 640
OWN = 10
PAD = 16
WIDE = 512
REST = D - WIDE
FIRST = 24
SECOND = 16
HALF = D // 2
NT = (((1,), (1,)), ((), ()))
CHUNKS = 4
PIECE = ROWS // CHUNKS


def kernel(
    img_hbm,
    base_hbm,
    feat_hbm,
    head_hbm,
    momentum_hbm,
    label_hbm,
    new_head_ref,
    new_momentum_ref,
    img_raw,
    head_ref,
    momentum_ref,
    img,
    tb,
    tf,
    tl,
    hb,
    pick,
    order,
    spread,
    feat_t,
    text_exact,
    text_unit,
    inv_norm,
    label_wide,
    unit_grad,
    grad_low,
    core_out,
    core_in,
    a_own,
    a_out,
    a_in,
    b_own,
    b_out,
    b_in,
    a2_own,
    a2_out,
    a2_in,
    b2_own,
    b2_out,
    b2_in,
    z_out,
    z_in,
    share,
    local_sem,
    up_send,
    up_recv,
    dn_send,
    dn_recv,
    text_send,
    text_recv,
    hz_send,
    hz_recv,
    hy_send,
    hy_recv,
    hx_send,
    hx_recv,
    hc_send,
    hc_recv,
    gc_send,
    gc_recv,
    ga_send,
    ga_recv,
    gb_send,
    gb_recv,
    gz_send,
    gz_recv,
    gs_send,
    gs_recv,
):
    dp = lax.axis_index("dp")
    rep = lax.axis_index("replica")
    z, yh, c = dp // 4, (dp // 2) % 2, dp % 2
    yl, x = rep // 4, rep % 4
    y = yl + 2 * yh

    def at(z2, y2, x2, c2):
        return (z2 * 4 + (y2 // 2) * 2 + c2, (y2 % 2) * 4 + x2)

    def to_z(k):
        return at((z + k) % NZ, y, x, c)

    def to_y(k):
        return at(z, (y + k) % 4, x, c)

    def to_x(k):
        return at(z, y, (x + k) % 4, c)

    to_core = at(z, y, x, 1 - c)

    def remote(src, dst, send, recv, device):
        return pltpu.make_async_remote_copy(
            src_ref=src, dst_ref=dst, send_sem=send, recv_sem=recv, device_id=device, device_id_type=MESH
        )

    loads = [
        pltpu.make_async_copy(img_hbm, img_raw, local_sem.at[0]),
        pltpu.make_async_copy(base_hbm, tb.at[0], local_sem.at[1]),
        pltpu.make_async_copy(feat_hbm, tf.at[0], local_sem.at[2]),
        pltpu.make_async_copy(label_hbm, tl.at[0], local_sem.at[3]),
        pltpu.make_async_copy(head_hbm, head_ref, local_sem.at[4]),
        pltpu.make_async_copy(momentum_hbm, momentum_ref, local_sem.at[5]),
    ]
    for load in loads:
        load.start()

    barrier = pltpu.get_barrier_semaphore()

    def greet(device):
        pl.semaphore_signal(barrier, inc=1, device_id=device, device_id_type=MESH)

    def greet_z(k, carry):
        greet(to_z(k))
        return carry

    lax.fori_loop(1, NZ, greet_z, 0)
    greet(to_core)
    for k in range(1, 4):
        greet(to_x(k))
        greet(to_y(k))
        greet(at(z, yh * 2 + (1 - yl), (x + k) % 4, c))

    loads[0].wait()
    wide = img_raw[...].astype(F32)
    img[0] = (wide * lax.rsqrt(jnp.sum(wide * wide, axis=1, keepdims=True) + norm_epsilon)).astype(BF16)

    def head_block(c2, x2, yl2, yh2, zh2):
        return (((c2 * 4 + x2) * 2 + yl2) * 2 + yh2) * 2 + zh2

    is_source = (z % 8) == rep
    own_block = head_block(c, x, yl, yh, z // 8)
    loads[4].wait()
    left, right = head_ref[:, :WIDE], head_ref[:, WIDE:]
    right = jnp.concatenate([right[: OWN // 2], right[OWN // 2 :]], axis=1)
    head_low = jnp.concatenate([left, right, jnp.zeros((1, WIDE), F32)], axis=0).astype(BF16)

    @pl.when(is_source)
    def _():
        hb[own_block] = head_low

    pl.semaphore_wait(barrier, 15 + 1 + 9)

    def head_z(k):
        block = hb.at[own_block]
        return remote(block, block, hz_send.at[k], hz_recv.at[z // 8], to_z(k))

    @pl.when(is_source)
    def _():
        def go(k, carry):
            head_z(k).start()
            return carry

        lax.fori_loop(1, NZ, go, 0)

    def text_copies(src, slot, device, first):
        return [
            remote(s, d, text_send.at[first + i], text_recv.at[first + i], device)
            for i, (s, d) in enumerate(zip(src, (tb.at[slot], tf.at[slot], tl.at[slot])))
        ]

    own_text = (base_hbm, feat_hbm, label_hbm)
    text_y = text_copies(own_text, 2, to_y(2), 0)
    text_c = text_copies(own_text, 1, to_core, 3)
    text_yc = text_copies((tb.at[2], tf.at[2], tl.at[2]), 3, to_core, 6)
    for copy in text_y:
        copy.start()

    def up(s, k):
        rows = pl.ds(k * PIECE, PIECE)
        src, dst = jnp.maximum(2 * s - 3, 0), 2 * s - 1
        return remote(img.at[src, rows], img.at[dst, rows], up_send.at[s, k], up_recv.at[s, k], to_z(1))

    def dn(s, k):
        rows = pl.ds(k * PIECE, PIECE)
        src, dst = 2 * s - 2, jnp.minimum(2 * s, 15)
        return remote(img.at[src, rows], img.at[dst, rows], dn_send.at[s, k], dn_recv.at[s, k], to_z(NZ - 1))

    for k in range(CHUNKS):
        up(1, k).start()
        dn(1, k).start()
    for copy in text_c:
        copy.start()

    def ring(s, chunks=range(CHUNKS)):
        for k in chunks:
            up(s, k).wait_recv()

            @pl.when((s < 7) | (k < CHUNKS // 2))
            def _():
                up(s + 1, k).start()

            dn(s, k).wait_recv()

            @pl.when((s < 7) | (k >= CHUNKS // 2))
            def _():
                dn(s + 1, k).start()

    early, late = range(CHUNKS // 2), range(CHUNKS // 2, CHUNKS)

    place = lax.broadcasted_iota(jnp.int32, (1, 64 * PAD), 1)
    block, row = place >> 4, place & 15
    source = ((block >> 3) & 3) + 4 * ((block >> 2) & 1) + 8 * (block & 1)
    first_row = (source * 4 + ((block >> 1) & 1) * 2 + (block >> 5)) * OWN
    packed = (row >= OWN) & (row < PAD - 1)
    row_of = lax.broadcasted_iota(jnp.int32, (K, 64 * PAD), 0)
    wanted = jnp.where(row < OWN, first_row + row, jnp.where(packed, first_row + row - OWN, -1))
    pick[0] = (row_of == wanted).astype(F32).astype(BF16)
    wanted = jnp.where(packed, first_row + row - OWN // 2, -1)
    pick[1] = (row_of == wanted).astype(F32).astype(BF16)

    place = lax.broadcasted_iota(jnp.int32, (K, 1), 0)
    block = (place * 6554) >> 16
    source = ((block >> 4) & 1) * 2 + ((block >> 2) & 1) + 4 * (block & 3)
    owner = source * 4 + ((block >> 3) & 1) * 2 + (c ^ 1 ^ (block >> 5))
    wanted = owner * OWN + place - block * OWN
    order[...] = (lax.broadcasted_iota(jnp.int32, (K, K), 1) == wanted).astype(F32).astype(BF16)

    def head_y(k):
        blocks = hb.at[pl.ds(head_block(c, x, yl, yh, 0), 2)]
        return remote(blocks, blocks, hy_send.at[k], hy_recv.at[k], to_y(k))

    def head_x(k):
        blocks = hb.at[pl.ds(head_block(c, x, 0, 0, 0), 8)]
        return remote(blocks, blocks, hx_send.at[k], hx_recv.at[k], to_x(k))

    all_mine = hb.at[pl.ds(c * 32, 32)]
    head_c = remote(all_mine, all_mine, hc_send, hc_recv, to_core)

    ring(1, early)
    for zh in range(2):

        @pl.when(z != rep + 8 * zh)
        def _():
            block = hb.at[head_block(c, x, yl, yh, zh)]
            remote(block, block, hz_send.at[0], hz_recv.at[zh], to_z(1)).wait_recv()

    for k in range(1, 4):
        head_y(k).start()
    ring(1, late)
    ring(2, early)
    for k in range(1, 4):
        head_y(k).wait_recv()
    for k in range(1, 4):
        head_x(k).start()
    ring(2, late)
    ring(3)
    for copy in text_y:
        copy.wait_recv()
    for copy in text_yc:
        copy.start()
    ring(4, early)

    for load in loads[1:4]:
        load.wait()
    for copy in text_c + text_yc:
        copy.wait_recv()
    features = tf[...].reshape(4 * ROWS, K)
    whole = jnp.dot(features, pick[0], preferred_element_type=F32)
    spread[0] = jnp.where(row < OWN, whole, 0.0).astype(BF16)
    spread[1] = jnp.where(row < OWN, 0.0, whole).astype(BF16)
    spread[2] = jnp.dot(features, pick[1], preferred_element_type=F32).astype(BF16)
    feat_t[...] = lax.dot_general(order[...], features, NT, preferred_element_type=F32).astype(BF16)
    diagonal = lax.broadcasted_iota(jnp.int32, (ROWS, ROWS), 0) == lax.broadcasted_iota(jnp.int32, (ROWS, ROWS), 1)
    for i in range(4):
        column = jnp.sum(jnp.where(diagonal, tl[i].astype(F32), 0.0), axis=1, keepdims=True)
        label_wide[pl.ds(i * ROWS, ROWS)] = jnp.broadcast_to(column, (ROWS, ROWS)).astype(jnp.int32)
    ring(4, late)
    for k in range(1, 4):
        head_x(k).wait_recv()
    head_c.start()
    ring(5, early)
    head_c.wait_recv()
    head_all = hb[...].reshape(64 * PAD, WIDE)
    for i in range(4):
        rows = pl.ds(i * ROWS, ROWS)
        left = jnp.dot(spread[0, rows], head_all, preferred_element_type=F32)
        right = jnp.dot(spread[1, rows], head_all[:, :REST], preferred_element_type=F32)
        right += jnp.dot(spread[2, rows], head_all[:, REST:], preferred_element_type=F32)
        emb = tb[i].astype(F32) + jnp.concatenate([left, right], axis=1)
        inv = lax.rsqrt(jnp.sum(emb * emb, axis=1, keepdims=True) + norm_epsilon)
        exact = emb * inv
        inv_norm[rows] = inv
        text_exact[rows] = exact
        text_unit[rows] = exact.astype(BF16)

    lane = lax.broadcasted_iota(jnp.int32, (1, ROWS), 1)

    def columns(z2):
        return ((z2 % NZ) * 4 + yh * 2 + c) * ROWS + lane

    def process(images, marks, fresh):
        for i in range(2):
            rows = pl.ds(i * 256, 256)
            raw = lax.dot_general(text_unit[rows], images, NT, preferred_element_type=F32)
            chance = 0.5 * jnp.tanh((0.5 * logit_scale) * raw + 0.5 * logit_bias) + 0.5
            labels = label_wide[rows]
            match = jnp.concatenate([(labels == m) for m in marks], axis=1)
            weights = jnp.where(match, chance - 1.0, chance).astype(BF16)
            grad = jnp.dot(weights, images, preferred_element_type=F32)
            if fresh:
                unit_grad[rows] = grad
            else:
                unit_grad[rows] += grad

    process(img[0], [columns(z)], True)
    ring(5, late)

    def pair(p, carry):
        @pl.when((p == 3) | (p == 6))
        def _():
            ring(5 + p // 3)

        images = img[pl.ds(2 * p - 1, 2)].reshape(2 * ROWS, D)
        process(images, [columns(z - p + NZ), columns(z + p)], False)
        return carry

    lax.fori_loop(1, 8, pair, 0)
    for k in range(CHUNKS // 2):
        up(8, k).wait_recv()
        dn(8, k + CHUNKS // 2).wait_recv()
    process(img[15], [columns(z + 8)], False)

    def drain():
        @pl.when(is_source)
        def _():
            def drain_head(k, carry):
                head_z(k).wait_send()
                return carry

            lax.fori_loop(1, NZ, drain_head, 0)

        for copy in text_y + text_c + text_yc + [head_c]:
            copy.wait_send()
        for k in range(1, 4):
            head_y(k).wait_send()
            head_x(k).wait_send()

        def drain_ring(s, carry):
            for k in range(CHUNKS):
                up(s, k).wait_send()
                dn(s, k).wait_send()
            return carry

        lax.fori_loop(1, 8, drain_ring, 0)
        for k in range(CHUNKS // 2):
            up(8, k).wait_send()
            dn(8, k + CHUNKS // 2).wait_send()

    for i in range(4):
        rows = pl.ds(i * ROWS, ROWS)
        exact, grad = text_exact[rows], unit_grad[rows]
        along = jnp.sum(exact * grad, axis=1, keepdims=True)
        grad_low[rows] = ((grad - exact * along) * (logit_scale * inv_norm[rows])).astype(BF16)

    def to_other(h):
        return remote(core_out.at[h], core_in.at[h], gc_send.at[h], gc_recv.at[h], to_core)

    for h in range(2):
        core_out[h] = jnp.dot(feat_t[pl.ds(h * 160, 160)], grad_low[...], preferred_element_type=F32).astype(BF16)
        to_other(h).start()
    for h in range(2):
        mine = jnp.dot(feat_t[pl.ds(320 + h * 160, 160)], grad_low[...], preferred_element_type=F32)
        to_other(h).wait_recv()
        mine += core_in[h].astype(F32)
        groups = [mine[k * 40 : (k + 1) * 40] for k in range(4)]
        first = jnp.concatenate([g[:FIRST] for g in groups], axis=0)
        for side in range(2):
            part = first[:, side * HALF : (side + 1) * HALF]
            a_own[2 * h + side] = part
            a_out[2 * h + side] = part.astype(BF16)
        for k in range(4):
            b_own[k, h] = groups[k][FIRST:]
            b_out[k, h] = groups[k][FIRST:].astype(BF16)

    def a_x(k):
        return remote(a_out.at[(x + k) % 4], a_in.at[k - 1], ga_send.at[0, k], ga_recv.at[0, k], to_x(k))

    def b_y(k):
        return remote(b_out.at[(y + k) % 4], b_in.at[k - 1], gb_send.at[0, k], gb_recv.at[0, k], to_y(k))

    def a_y(k):
        return remote(a2_out.at[(y + k) % 4], a2_in.at[k - 1], ga_send.at[1, k], ga_recv.at[1, k], to_y(k))

    def b_x(k):
        return remote(b2_out.at[(x + k) % 4], b2_in.at[k - 1], gb_send.at[1, k], gb_recv.at[1, k], to_x(k))

    for k in (2, 1, 3):
        a_x(k).start()
        b_y(k).start()
    drain()
    total = b_own[y]
    for k in (1, 3, 2):
        b_y(k).wait_recv()
        total += b_in[k - 1].astype(F32)
    for h in range(2):
        for side in range(2):
            part = total[h, :, side * HALF : (side + 1) * HALF]
            b2_own[2 * h + side] = part
            b2_out[2 * h + side] = part.astype(BF16)
    for k in (2, 1, 3):
        b_x(k).start()
    total = a_own[x]
    for k in (1, 3, 2):
        a_x(k).wait_recv()
        total += a_in[k - 1].astype(F32)
    for k in range(4):
        part = total[k * FIRST : (k + 1) * FIRST]
        a2_own[k] = part
        a2_out[k] = jnp.concatenate([part, jnp.zeros((32 - FIRST, HALF), F32)], axis=0).astype(BF16)
    for k in (2, 1, 3):
        a_y(k).start()
    second = b2_own[x]
    for k in (1, 3, 2):
        b_x(k).wait_recv()
        second += b2_in[k - 1].astype(F32)
    first = a2_own[y]
    for k in (1, 3, 2):
        a_y(k).wait_recv()
        first += a2_in[k - 1, :FIRST].astype(F32)
    total = jnp.concatenate([first, second], axis=0)
    for j in range(4):
        part = total[j * OWN : (j + 1) * OWN]
        thirds = [part[:, i * 128 : (i + 1) * 128] for i in range(3)] + [jnp.zeros((2, 128), F32)]
        z_out[j] = jnp.concatenate(thirds, axis=0).astype(BF16)

    group = 2 * (x // 2) + yl

    def to_z_part(j):
        k = (group + 4 * j - z + NZ) % NZ
        return remote(z_out.at[j], z_in.at[k], gz_send.at[j], gz_recv.at[k], to_z(k))

    for j in range(4):

        @pl.when(z != group + 4 * j)
        def _():
            to_z_part(j).start()

    is_owner = (z % 4) == group
    side = x % 2

    def to_share(i):
        rep2 = (rep + i) % 8
        device = (dp, rep2)
        return remote(share.at[side], share.at[side], gs_send.at[i], gs_recv.at[side], device)

    @pl.when(is_owner)
    def _():
        z_in[0] = z_out[z // 4]
        for k in range(1, NZ):
            remote(z_out.at[0], z_in.at[k], gz_send.at[0], gz_recv.at[k], to_z(1)).wait_recv()
        share[side] = jnp.sum(z_in[...].astype(F32), axis=0)
        for i in range(1, 8):
            to_share(i).start()

    for s in range(2):

        @pl.when(jnp.logical_not(is_owner & (side == s)))
        def _():
            remote(share.at[s], share.at[s], gs_send.at[0], gs_recv.at[s], to_x(1)).wait_recv()

    pieces = [share[s, i * OWN : (i + 1) * OWN] for s in range(2) for i in range(3)]
    head_grad = jnp.concatenate(pieces, axis=1) * (1.0 / 8.0)
    loads[5].wait()
    momentum = momentum_decay * momentum_ref[...] + (1.0 - momentum_decay) * head_grad
    new_momentum_ref[...] = momentum
    new_head_ref[...] = head_ref[...] - outer_rate * ((1.0 - blend_weight) * head_grad + blend_weight * momentum)

    for k in range(1, 4):
        a_x(k).wait_send()
        b_y(k).wait_send()
        a_y(k).wait_send()
        b_x(k).wait_send()
    for h in range(2):
        to_other(h).wait_send()
    for j in range(4):

        @pl.when(z != group + 4 * j)
        def _():
            to_z_part(j).wait_send()

    @pl.when(is_owner)
    def _():
        for i in range(1, 8):
            to_share(i).wait_send()


def per_device(img_emb, txt_base, txt_feat, head, momentum, positive_image):
    vmem = pl.BlockSpec(memory_space=pltpu.VMEM)
    hbm = pl.BlockSpec(memory_space=pl.ANY)
    dma = pltpu.SemaphoreType.DMA
    texts = 4 * ROWS
    out = jax.ShapeDtypeStruct((OWN, D), F32)
    return pl.pallas_call(
        kernel,
        out_shape=(out, out),
        in_specs=[hbm] * 6,
        out_specs=(vmem, vmem),
        scratch_shapes=[
            pltpu.VMEM((ROWS, D), BF16),
            pltpu.VMEM((OWN, D), F32),
            pltpu.VMEM((OWN, D), F32),
            pltpu.VMEM((NZ, ROWS, D), BF16),
            pltpu.VMEM((4, ROWS, D), BF16),
            pltpu.VMEM((4, ROWS, K), BF16),
            pltpu.VMEM((4, 1, ROWS), jnp.int32),
            pltpu.VMEM((64, PAD, WIDE), BF16),
            pltpu.VMEM((2, K, 64 * PAD), BF16),
            pltpu.VMEM((K, K), BF16),
            pltpu.VMEM((3, texts, 64 * PAD), BF16),
            pltpu.VMEM((K, texts), BF16),
            pltpu.VMEM((texts, D), F32),
            pltpu.VMEM((texts, D), BF16),
            pltpu.VMEM((texts, 1), F32),
            pltpu.VMEM((texts, ROWS), jnp.int32),
            pltpu.VMEM((texts, D), F32),
            pltpu.VMEM((texts, D), BF16),
            pltpu.VMEM((2, 160, D), BF16),
            pltpu.VMEM((2, 160, D), BF16),
            pltpu.VMEM((4, 4 * FIRST, HALF), F32),
            pltpu.VMEM((4, 4 * FIRST, HALF), BF16),
            pltpu.VMEM((3, 4 * FIRST, HALF), BF16),
            pltpu.VMEM((4, 2, SECOND, D), F32),
            pltpu.VMEM((4, 2, SECOND, D), BF16),
            pltpu.VMEM((3, 2, SECOND, D), BF16),
            pltpu.VMEM((4, FIRST, HALF), F32),
            pltpu.VMEM((4, 32, HALF), BF16),
            pltpu.VMEM((3, 32, HALF), BF16),
            pltpu.VMEM((4, SECOND, HALF), F32),
            pltpu.VMEM((4, SECOND, HALF), BF16),
            pltpu.VMEM((3, SECOND, HALF), BF16),
            pltpu.VMEM((4, 32, 128), BF16),
            pltpu.VMEM((NZ, 32, 128), BF16),
            pltpu.VMEM((2, 32, 128), F32),
            dma((6,)),
            dma((9, CHUNKS)),
            dma((9, CHUNKS)),
            dma((9, CHUNKS)),
            dma((9, CHUNKS)),
            dma((9,)),
            dma((9,)),
            dma((NZ,)),
            dma((2,)),
            dma((4,)),
            dma((4,)),
            dma((4,)),
            dma((4,)),
            dma,
            dma,
            dma((2,)),
            dma((2,)),
            dma((2, 4)),
            dma((2, 4)),
            dma((2, 4)),
            dma((2, 4)),
            dma((4,)),
            dma((NZ,)),
            dma((8,)),
            dma((2,)),
        ],
        compiler_params=pltpu.CompilerParams(
            collective_id=0, has_side_effects=True, vmem_limit_bytes=63 * 1024 * 1024
        ),
        cost_estimate=pl.CostEstimate(flops=8_000_000_000, bytes_accessed=2_000_000, transcendentals=1_100_000),
        name="contrastive_step",
    )(img_emb[0], txt_base[0], txt_feat[0], head, momentum, positive_image)


def solution(mesh):
    placed = (
        P("replica", "dp", None),
        P("replica", "dp", None),
        P("replica", "dp", None),
        P("dp", None),
        P("dp", None),
        P("replica", "dp"),
    )
    return jax.shard_map(
        per_device,
        mesh=mesh,
        in_specs=placed,
        out_specs=(P("dp", None), P("dp", None)),
        check_vma=False,
    )
```

```python
import functools

import jax
import jax.numpy as jnp
from jax import lax
from jax.experimental import pallas as pl
from jax.experimental.pallas import tpu as pltpu
from jax.sharding import PartitionSpec as P

MESH = pl.DeviceIdType.MESH
F32 = jnp.float32
BF16 = jnp.bfloat16

logit_scale = 10.0
logit_bias = -3.0
norm_epsilon = 1e-06
momentum_decay = 0.9
blend_weight = 0.7
outer_rate = 0.7

NZ = 16
ROWS = 128
D = 768
K = 640
OWN = 10
PAD = 16
WIDE = 512
REST = D - WIDE
FIRST = 24
SECOND = 16
HALF = D // 2
NT = (((1,), (1,)), ((), ()))
CHUNKS = 4
PIECE = ROWS // CHUNKS


def kernel(
    img_hbm,
    base_hbm,
    feat_hbm,
    head_hbm,
    label_hbm,
    head_grad_ref,
    img_raw,
    head_ref,
    img,
    tb,
    tf,
    tl,
    hb,
    pick,
    order,
    spread,
    feat_t,
    text_exact,
    text_unit,
    inv_norm,
    label_wide,
    unit_grad,
    grad_low,
    grad_in,
    partial,
    a_own,
    a_out,
    a_in,
    b_own,
    b_out,
    b_in,
    a2_own,
    a2_out,
    a2_in,
    b2_own,
    b2_out,
    b2_in,
    z_out,
    z_in,
    share,
    local_sem,
    up_send,
    up_recv,
    dn_send,
    dn_recv,
    text_send,
    text_recv,
    hz_send,
    hz_recv,
    hy_send,
    hy_recv,
    hx_send,
    hx_recv,
    hc_send,
    hc_recv,
    gc_send,
    gc_recv,
    ga_send,
    ga_recv,
    gb_send,
    gb_recv,
    gz_send,
    gz_recv,
    gs_send,
    gs_recv,
):
    dp = lax.axis_index("dp")
    rep = lax.axis_index("replica")
    z, yh, c = dp // 4, (dp // 2) % 2, dp % 2
    yl, x = rep // 4, rep % 4
    y = yl + 2 * yh

    def at(z2, y2, x2, c2):
        return (z2 * 4 + (y2 // 2) * 2 + c2, (y2 % 2) * 4 + x2)

    def to_z(k):
        return at((z + k) % NZ, y, x, c)

    def to_y(k):
        return at(z, (y + k) % 4, x, c)

    def to_x(k):
        return at(z, y, (x + k) % 4, c)

    to_core = at(z, y, x, 1 - c)

    def remote(src, dst, send, recv, device):
        return pltpu.make_async_remote_copy(
            src_ref=src, dst_ref=dst, send_sem=send, recv_sem=recv, device_id=device, device_id_type=MESH
        )

    loads = [
        pltpu.make_async_copy(img_hbm, img_raw, local_sem.at[0]),
        pltpu.make_async_copy(base_hbm, tb.at[0], local_sem.at[1]),
        pltpu.make_async_copy(feat_hbm, tf.at[0], local_sem.at[2]),
        pltpu.make_async_copy(label_hbm, tl.at[0], local_sem.at[3]),
        pltpu.make_async_copy(head_hbm, head_ref, local_sem.at[4]),
    ]
    for load in loads:
        load.start()

    barrier = pltpu.get_barrier_semaphore()

    def greet(device):
        pl.semaphore_signal(barrier, inc=1, device_id=device, device_id_type=MESH)

    head_z0 = (rep + 4 * c) % 8
    is_source = (z % 8) == head_z0
    greet(to_z(1))
    greet(to_z(NZ - 1))
    greet(to_core)
    for k in range(1, 4):
        greet(to_x(k))
        greet(to_y(k))
        greet(at(z, yh * 2 + (1 - yl), (x + k) % 4, c))
    for zh in range(2):
        away = (head_z0 + 8 * zh - z + NZ) % NZ

        @pl.when((away > 1) & (away < NZ - 1))
        def _():
            greet(to_z(away))

    loads[0].wait()
    wide = img_raw[...].astype(F32)
    img[0] = (wide * lax.rsqrt(jnp.sum(wide * wide, axis=1, keepdims=True) + norm_epsilon)).astype(BF16)

    def head_block(c2, x2, yl2, yh2, zh2):
        return (((c2 * 4 + x2) * 2 + yl2) * 2 + yh2) * 2 + zh2

    own_block = head_block(c, x, yl, yh, z // 8)
    loads[4].wait()
    left, right = head_ref[:, :WIDE], head_ref[:, WIDE:]
    right = jnp.concatenate([right[: OWN // 2], right[OWN // 2 :]], axis=1)
    head_low = jnp.concatenate([left, right, jnp.zeros((1, WIDE), F32)], axis=0).astype(BF16)

    @pl.when(is_source)
    def _():
        hb[own_block] = head_low

    pl.semaphore_wait(barrier, jnp.where(is_source, 15 + 1 + 9, 2 + 1 + 9))

    def head_z(k):
        block = hb.at[own_block]
        return remote(block, block, hz_send.at[k], hz_recv.at[z // 8], to_z(k))

    @pl.when(is_source)
    def _():
        def go(k, carry):
            head_z(k).start()
            return carry

        lax.fori_loop(1, NZ, go, 0)

    def text_copies(src, slot, device, first):
        return [
            remote(s, d, text_send.at[first + i], text_recv.at[first + i], device)
            for i, (s, d) in enumerate(zip(src, (tb.at[slot], tf.at[slot], tl.at[slot])))
        ]

    own_text = (base_hbm, feat_hbm, label_hbm)
    text_y = text_copies(own_text, 2, to_y(2), 0)
    text_c = text_copies(own_text, 1, to_core, 3)
    text_yc = text_copies((tb.at[2], tf.at[2], tl.at[2]), 3, to_core, 6)
    for copy in text_y:
        copy.start()

    def up(s, k):
        rows = pl.ds(k * PIECE, PIECE)
        src, dst = jnp.maximum(2 * s - 3, 0), 2 * s - 1
        return remote(img.at[src, rows], img.at[dst, rows], up_send.at[s, k], up_recv.at[s, k], to_z(1))

    def dn(s, k):
        rows = pl.ds(k * PIECE, PIECE)
        src, dst = 2 * s - 2, jnp.minimum(2 * s, 15)
        return remote(img.at[src, rows], img.at[dst, rows], dn_send.at[s, k], dn_recv.at[s, k], to_z(NZ - 1))

    for k in range(CHUNKS):
        up(1, k).start()
        dn(1, k).start()
    for copy in text_c:
        copy.start()

    def ring(s, chunks=range(CHUNKS)):
        for k in chunks:
            up(s, k).wait_recv()

            @pl.when((s < 7) | (k < CHUNKS // 2))
            def _():
                up(s + 1, k).start()

            dn(s, k).wait_recv()

            @pl.when((s < 7) | (k >= CHUNKS // 2))
            def _():
                dn(s + 1, k).start()

    early, late = range(CHUNKS // 2), range(CHUNKS // 2, CHUNKS)

    place = lax.broadcasted_iota(jnp.int32, (1, 64 * PAD), 1)
    block, row = place >> 4, place & 15
    source = ((block >> 3) & 3) + 4 * (((block >> 2) ^ (block >> 5)) & 1) + 8 * (block & 1)
    first_row = (source * 4 + ((block >> 1) & 1) * 2 + (block >> 5)) * OWN
    packed = (row >= OWN) & (row < PAD - 1)
    row_of = lax.broadcasted_iota(jnp.int32, (K, 64 * PAD), 0)
    wanted = jnp.where(row < OWN, first_row + row, jnp.where(packed, first_row + row - OWN, -1))
    pick[0] = (row_of == wanted).astype(F32).astype(BF16)
    wanted = jnp.where(packed, first_row + row - OWN // 2, -1)
    pick[1] = (row_of == wanted).astype(F32).astype(BF16)

    place = lax.broadcasted_iota(jnp.int32, (K // 2, 1), 0)
    block = (place * 6554) >> 16
    source = ((block >> 4) & 1) * 2 + ((block >> 2) & 1) + 4 * (block & 3)
    owner = source * 4 + ((block >> 3) & 1) * 2 + c
    wanted = owner * OWN + place - block * OWN
    order[...] = (lax.broadcasted_iota(jnp.int32, (K // 2, K), 1) == wanted).astype(F32).astype(BF16)

    def head_y(k):
        blocks = hb.at[pl.ds(head_block(c, x, yl, yh, 0), 2)]
        return remote(blocks, blocks, hy_send.at[k], hy_recv.at[k], to_y(k))

    def head_x(k):
        blocks = hb.at[pl.ds(head_block(c, x, 0, 0, 0), 8)]
        return remote(blocks, blocks, hx_send.at[k], hx_recv.at[k], to_x(k))

    all_mine = hb.at[pl.ds(c * 32, 32)]
    head_c = remote(all_mine, all_mine, hc_send, hc_recv, to_core)

    ring(1)
    for zh in range(2):

        @pl.when(z != head_z0 + 8 * zh)
        def _():
            block = hb.at[head_block(c, x, yl, yh, zh)]
            remote(block, block, hz_send.at[0], hz_recv.at[zh], to_z(1)).wait_recv()

    for k in range(1, 4):
        head_y(k).start()
    ring(2)
    for k in range(1, 4):
        head_y(k).wait_recv()
    for k in (2, 1, 3):
        head_x(k).start()
    ring(3)
    ring(4, early)
    for copy in text_y:
        copy.wait_recv()
    for copy in text_yc:
        copy.start()
    ring(4, late)

    for load in loads[1:4]:
        load.wait()
    for copy in text_c + text_yc:
        copy.wait_recv()
    features = tf[...].reshape(4 * ROWS, K)
    whole = jnp.dot(features, pick[0], preferred_element_type=F32)
    spread[0] = jnp.where(row < OWN, whole, 0.0).astype(BF16)
    spread[1] = jnp.where(row < OWN, 0.0, whole).astype(BF16)
    spread[2] = jnp.dot(features, pick[1], preferred_element_type=F32).astype(BF16)
    feat_t[...] = lax.dot_general(order[...], features, NT, preferred_element_type=F32).astype(BF16)
    diagonal = lax.broadcasted_iota(jnp.int32, (ROWS, ROWS), 0) == lax.broadcasted_iota(jnp.int32, (ROWS, ROWS), 1)
    for i in range(4):
        column = jnp.sum(jnp.where(diagonal, tl[i].astype(F32), 0.0), axis=1, keepdims=True)
        label_wide[pl.ds(i * ROWS, ROWS)] = jnp.broadcast_to(column, (ROWS, ROWS)).astype(jnp.int32)
    ring(5)
    for k in range(1, 4):
        head_x(k).wait_recv()
    head_c.start()
    ring(6, early)
    head_c.wait_recv()
    head_all = hb[...].reshape(64 * PAD, WIDE)
    for i in range(4):
        rows = pl.ds(i * ROWS, ROWS)
        left = jnp.dot(spread[0, rows], head_all, preferred_element_type=F32)
        right = jnp.dot(spread[1, rows], head_all[:, :REST], preferred_element_type=F32)
        right += jnp.dot(spread[2, rows], head_all[:, REST:], preferred_element_type=F32)
        emb = tb[i].astype(F32) + jnp.concatenate([left, right], axis=1)
        inv = lax.rsqrt(jnp.sum(emb * emb, axis=1, keepdims=True) + norm_epsilon)
        exact = emb * inv
        inv_norm[rows] = inv
        text_exact[rows] = exact
        text_unit[rows] = exact.astype(BF16)

    lane = lax.broadcasted_iota(jnp.int32, (1, ROWS), 1)

    def columns(z2):
        return ((z2 % NZ) * 4 + yh * 2 + c) * ROWS + lane

    def process(first, blocks, marks, fresh=False):
        images = img[pl.ds(first, blocks)].reshape(blocks * ROWS, D)
        halves = [pl.ds(i * 256, 256) for i in range(2)]
        raws = [lax.dot_general(text_unit[rows], images, NT, preferred_element_type=F32) for rows in halves]
        for rows, raw in zip(halves, raws):
            chance = 0.5 * jnp.tanh((0.5 * logit_scale) * raw + 0.5 * logit_bias) + 0.5
            labels = label_wide[rows]
            match = jnp.concatenate([(labels == columns(z + m + NZ)) for m in marks], axis=1)
            weights = jnp.where(match, chance - 1.0, chance).astype(BF16)
            grad = jnp.dot(weights, images, preferred_element_type=F32)
            if fresh:
                unit_grad[rows] = grad
            else:
                unit_grad[rows] += grad

    ring(6, late)
    process(0, 4, (0, -1, 1, -2), True)
    ring(7, early)
    process(4, 4, (2, -3, 3, -4))
    ring(7, late)
    process(8, 4, (4, -5, 5, -6))
    process(12, 3, (6, -7, 7))
    for k in range(CHUNKS // 2):
        up(8, k).wait_recv()
        dn(8, k + CHUNKS // 2).wait_recv()
    process(15, 1, (8,))

    def drain():
        @pl.when(is_source)
        def _():
            def drain_head(k, carry):
                head_z(k).wait_send()
                return carry

            lax.fori_loop(1, NZ, drain_head, 0)

        for copy in text_y + text_c + text_yc + [head_c]:
            copy.wait_send()
        for k in range(1, 4):
            head_y(k).wait_send()
            head_x(k).wait_send()

        def drain_ring(s, carry):
            for k in range(CHUNKS):
                up(s, k).wait_send()
                dn(s, k).wait_send()
            return carry

        lax.fori_loop(1, 8, drain_ring, 0)
        for k in range(CHUNKS // 2):
            up(8, k).wait_send()
            dn(8, k + CHUNKS // 2).wait_send()

    def to_other(i):
        rows, there = pl.ds(i * ROWS, ROWS), pl.ds((i ^ 1) * ROWS, ROWS)
        return remote(grad_low.at[rows], grad_in.at[there], gc_send.at[i], gc_recv.at[i], to_core)

    for i in range(4):
        rows = pl.ds(i * ROWS, ROWS)
        exact, grad = text_exact[rows], unit_grad[rows]
        along = jnp.sum(exact * grad, axis=1, keepdims=True)
        grad_low[rows] = ((grad - exact * along) * (logit_scale * inv_norm[rows])).astype(BF16)
        to_other(i).start()

    def a_x(k):
        return remote(a_out.at[(x + k) % 4], a_in.at[k - 1], ga_send.at[0, k], ga_recv.at[0], to_x(k))

    def b_y(k):
        return remote(b_out.at[(y + k) % 4], b_in.at[k - 1], gb_send.at[0, k], gb_recv.at[0], to_y(k))

    def a_y(k):
        return remote(a2_out.at[(y + k) % 4], a2_in.at[k - 1], ga_send.at[1, k], ga_recv.at[1], to_y(k))

    def b_x(k):
        return remote(b2_out.at[(x + k) % 4], b2_in.at[k - 1], gb_send.at[1, k], gb_recv.at[1], to_x(k))

    def all_in(ref, sem):
        remote(ref, ref, ga_send.at[0, 0], sem, to_x(1)).wait_recv()

    for h in range(2):
        partial[h] = jnp.dot(feat_t[pl.ds(h * 160, 160)], grad_low[...], preferred_element_type=F32)
    for i in range(4):
        to_other(i).wait_recv()
    for h in range(2):
        mine = partial[h] + jnp.dot(feat_t[pl.ds(h * 160, 160)], grad_in[...], preferred_element_type=F32)
        groups = [mine[k * 40 : (k + 1) * 40] for k in range(4)]
        first = jnp.concatenate([g[:FIRST] for g in groups], axis=0)
        for side in range(2):
            part = first[:, side * HALF : (side + 1) * HALF]
            a_own[2 * h + side] = part
            a_out[2 * h + side] = part.astype(BF16)
        for k in (2, 1, 3):

            @pl.when((x + k) % 4 // 2 == h)
            def _():
                a_x(k).start()

        for k in range(4):
            b_own[k, h] = groups[k][FIRST:]
            b_out[k, h] = groups[k][FIRST:].astype(BF16)

    for k in (2, 1, 3):
        b_y(k).start()
    drain()
    all_in(b_in, gb_recv.at[0])
    total = b_own[y]
    for k in range(3):
        total += b_in[k].astype(F32)
    for h in range(2):
        for side in range(2):
            part = total[h, :, side * HALF : (side + 1) * HALF]
            b2_own[2 * h + side] = part
            b2_out[2 * h + side] = part.astype(BF16)
    for k in (2, 1, 3):
        b_x(k).start()
    all_in(a_in, ga_recv.at[0])
    total = a_own[x]
    for k in range(3):
        total += a_in[k].astype(F32)
    for k in range(4):
        part = total[k * FIRST : (k + 1) * FIRST]
        a2_own[k] = part
        a2_out[k] = jnp.concatenate([part, jnp.zeros((32 - FIRST, HALF), F32)], axis=0).astype(BF16)
    for k in (2, 1, 3):
        a_y(k).start()
    all_in(b2_in, gb_recv.at[1])
    second = b2_own[x]
    for k in range(3):
        second += b2_in[k].astype(F32)
    all_in(a2_in, ga_recv.at[1])
    first = a2_own[y]
    for k in range(3):
        first += a2_in[k, :FIRST].astype(F32)
    total = jnp.concatenate([first, second], axis=0)
    for j in range(4):
        part = total[j * OWN : (j + 1) * OWN]
        thirds = [part[:, i * 128 : (i + 1) * 128] for i in range(3)] + [jnp.zeros((2, 128), F32)]
        z_out[j] = jnp.concatenate(thirds, axis=0).astype(BF16)

    group = 2 * (x // 2) + yl

    def to_z_part(j):
        k = (group + 4 * j - z + NZ) % NZ
        return remote(z_out.at[j], z_in.at[k], gz_send.at[j], gz_recv, to_z(k))

    for j in range(4):

        @pl.when(z != group + 4 * j)
        def _():
            to_z_part(j).start()

    is_owner = (z % 4) == group
    side = x % 2

    def to_share(i):
        rep2 = (rep + i) % 8
        device = (dp, rep2)
        return remote(share.at[side], share.at[side], gs_send.at[i], gs_recv.at[side], device)

    @pl.when(is_owner)
    def _():
        z_in[0] = z_out[z // 4]
        others = z_in.at[pl.ds(1, NZ - 1)]
        remote(others, others, gz_send.at[0], gz_recv, to_z(1)).wait_recv()
        share[side] = jnp.sum(z_in[...].astype(F32), axis=0)
        for i in range(1, 8):
            to_share(i).start()

    for s in range(2):

        @pl.when(jnp.logical_not(is_owner & (side == s)))
        def _():
            remote(share.at[s], share.at[s], gs_send.at[0], gs_recv.at[s], to_x(1)).wait_recv()

    pieces = [share[s, i * OWN : (i + 1) * OWN] for s in range(2) for i in range(3)]
    head_grad_ref[...] = jnp.concatenate(pieces, axis=1) * (1.0 / 8.0)

    for k in range(1, 4):
        a_x(k).wait_send()
        b_y(k).wait_send()
        a_y(k).wait_send()
        b_x(k).wait_send()
    for i in range(4):
        to_other(i).wait_send()
    for j in range(4):

        @pl.when(z != group + 4 * j)
        def _():
            to_z_part(j).wait_send()

    @pl.when(is_owner)
    def _():
        for i in range(1, 8):
            to_share(i).wait_send()


def per_device(img_emb, txt_base, txt_feat, head, momentum, positive_image):
    vmem = pl.BlockSpec(memory_space=pltpu.VMEM)
    hbm = pl.BlockSpec(memory_space=pl.ANY)
    dma = pltpu.SemaphoreType.DMA
    texts = 4 * ROWS
    out = jax.ShapeDtypeStruct((OWN, D), F32)
    head_grad = pl.pallas_call(
        kernel,
        out_shape=out,
        in_specs=[hbm] * 5,
        out_specs=vmem,
        scratch_shapes=[
            pltpu.VMEM((ROWS, D), BF16),
            pltpu.VMEM((OWN, D), F32),
            pltpu.VMEM((NZ, ROWS, D), BF16),
            pltpu.VMEM((4, ROWS, D), BF16),
            pltpu.VMEM((4, ROWS, K), BF16),
            pltpu.VMEM((4, 1, ROWS), jnp.int32),
            pltpu.VMEM((64, PAD, WIDE), BF16),
            pltpu.VMEM((2, K, 64 * PAD), BF16),
            pltpu.VMEM((K // 2, K), BF16),
            pltpu.VMEM((3, texts, 64 * PAD), BF16),
            pltpu.VMEM((K // 2, texts), BF16),
            pltpu.VMEM((texts, D), F32),
            pltpu.VMEM((texts, D), BF16),
            pltpu.VMEM((texts, 1), F32),
            pltpu.VMEM((texts, ROWS), jnp.int32),
            pltpu.VMEM((texts, D), F32),
            pltpu.VMEM((texts, D), BF16),
            pltpu.VMEM((texts, D), BF16),
            pltpu.VMEM((2, 160, D), F32),
            pltpu.VMEM((4, 4 * FIRST, HALF), F32),
            pltpu.VMEM((4, 4 * FIRST, HALF), BF16),
            pltpu.VMEM((3, 4 * FIRST, HALF), BF16),
            pltpu.VMEM((4, 2, SECOND, D), F32),
            pltpu.VMEM((4, 2, SECOND, D), BF16),
            pltpu.VMEM((3, 2, SECOND, D), BF16),
            pltpu.VMEM((4, FIRST, HALF), F32),
            pltpu.VMEM((4, 32, HALF), BF16),
            pltpu.VMEM((3, 32, HALF), BF16),
            pltpu.VMEM((4, SECOND, HALF), F32),
            pltpu.VMEM((4, SECOND, HALF), BF16),
            pltpu.VMEM((3, SECOND, HALF), BF16),
            pltpu.VMEM((4, 32, 128), BF16),
            pltpu.VMEM((NZ, 32, 128), BF16),
            pltpu.VMEM((2, 32, 128), F32),
            dma((5,)),
            dma((9, CHUNKS)),
            dma((9, CHUNKS)),
            dma((9, CHUNKS)),
            dma((9, CHUNKS)),
            dma((9,)),
            dma((9,)),
            dma((NZ,)),
            dma((2,)),
            dma((4,)),
            dma((4,)),
            dma((4,)),
            dma((4,)),
            dma,
            dma,
            dma((4,)),
            dma((4,)),
            dma((2, 4)),
            dma((2,)),
            dma((2, 4)),
            dma((2,)),
            dma((4,)),
            dma,
            dma((8,)),
            dma((2,)),
        ],
        compiler_params=pltpu.CompilerParams(
            collective_id=0, has_side_effects=True, vmem_limit_bytes=63 * 1024 * 1024
        ),
        cost_estimate=pl.CostEstimate(flops=8_000_000_000, bytes_accessed=2_000_000, transcendentals=1_100_000),
        name="contrastive_step",
    )(img_emb[0], txt_base[0], txt_feat[0], head, positive_image)
    new_momentum = momentum_decay * momentum + (1.0 - momentum_decay) * head_grad
    new_head = head - outer_rate * ((1.0 - blend_weight) * head_grad + blend_weight * new_momentum)
    return (new_head, new_momentum)


def solution(mesh):
    placed = (
        P("replica", "dp", None),
        P("replica", "dp", None),
        P("replica", "dp", None),
        P("dp", None),
        P("dp", None),
        P("replica", "dp"),
    )
    return jax.shard_map(
        per_device,
        mesh=mesh,
        in_specs=placed,
        out_specs=(P("dp", None), P("dp", None)),
        check_vma=False,
    )
```

```python
import functools

import jax
import jax.numpy as jnp
from jax import lax
from jax.experimental import pallas as pl
from jax.experimental.pallas import tpu as pltpu
from jax.sharding import PartitionSpec as P

MESH = pl.DeviceIdType.MESH
F32 = jnp.float32
BF16 = jnp.bfloat16

logit_scale = 10.0
logit_bias = -3.0
norm_epsilon = 1e-06
momentum_decay = 0.9
blend_weight = 0.7
outer_rate = 0.7

NZ = 16
ROWS = 128
D = 768
K = 640
OWN = 10
PAD = 16
WIDE = 512
REST = D - WIDE
FIRST = 24
SECOND = 16
HALF = D // 2
NT = (((1,), (1,)), ((), ()))
CHUNKS = 4
PIECE = ROWS // CHUNKS


def kernel(
    img_hbm,
    base_hbm,
    feat_hbm,
    head_hbm,
    label_hbm,
    head_grad_ref,
    img_raw,
    head_ref,
    img,
    tb,
    tf,
    tl,
    hb,
    pick,
    order,
    spread,
    feat_t,
    text_exact,
    text_unit,
    inv_norm,
    label_wide,
    unit_grad,
    grad_low,
    grad_in,
    partial,
    piece,
    x_out,
    x_in,
    x_far_out,
    x_far_in,
    y_out,
    y_in,
    y_far_out,
    y_far_in,
    x2_out,
    x2_in,
    x2_far_out,
    x2_far_in,
    y2_out,
    y2_in,
    y2_far_out,
    y2_far_in,
    z_out,
    z_in,
    share,
    local_sem,
    up_send,
    up_recv,
    dn_send,
    dn_recv,
    text_send,
    text_recv,
    hz_send,
    hz_recv,
    hy_send,
    hy_recv,
    hx_send,
    hx_recv,
    hc_send,
    hc_recv,
    gc_send,
    gc_recv,
    ga_send,
    ga_recv,
    gb_send,
    gb_recv,
    gz_send,
    gz_recv,
    gs_send,
    gs_recv,
):
    dp = lax.axis_index("dp")
    rep = lax.axis_index("replica")
    z, yh, c = dp // 4, (dp // 2) % 2, dp % 2
    yl, x = rep // 4, rep % 4
    y = yl + 2 * yh

    def at(z2, y2, x2, c2):
        return (z2 * 4 + (y2 // 2) * 2 + c2, (y2 % 2) * 4 + x2)

    def to_z(k):
        return at((z + k) % NZ, y, x, c)

    def to_y(k):
        return at(z, (y + k) % 4, x, c)

    def to_x(k):
        return at(z, y, (x + k) % 4, c)

    to_core = at(z, y, x, 1 - c)

    def remote(src, dst, send, recv, device):
        return pltpu.make_async_remote_copy(
            src_ref=src, dst_ref=dst, send_sem=send, recv_sem=recv, device_id=device, device_id_type=MESH
        )

    loads = [
        pltpu.make_async_copy(img_hbm, img_raw, local_sem.at[0]),
        pltpu.make_async_copy(base_hbm, tb.at[0], local_sem.at[1]),
        pltpu.make_async_copy(feat_hbm, tf.at[0], local_sem.at[2]),
        pltpu.make_async_copy(label_hbm, tl.at[0], local_sem.at[3]),
        pltpu.make_async_copy(head_hbm, head_ref, local_sem.at[4]),
    ]
    for load in loads:
        load.start()

    barrier = pltpu.get_barrier_semaphore()

    def greet(device):
        pl.semaphore_signal(barrier, inc=1, device_id=device, device_id_type=MESH)

    head_z0 = (rep + 4 * c) % 8
    is_source = (z % 8) == head_z0
    greet(to_z(1))
    greet(to_z(NZ - 1))
    greet(to_core)
    for k in range(1, 4):
        greet(to_x(k))
        greet(to_y(k))
        greet(at(z, yh * 2 + (1 - yl), (x + k) % 4, c))
    for zh in range(2):
        away = (head_z0 + 8 * zh - z + NZ) % NZ

        @pl.when((away > 1) & (away < NZ - 1))
        def _():
            greet(to_z(away))

    loads[0].wait()
    wide = img_raw[...].astype(F32)
    img[0] = (wide * lax.rsqrt(jnp.sum(wide * wide, axis=1, keepdims=True) + norm_epsilon)).astype(BF16)

    def head_block(c2, x2, yl2, yh2, zh2):
        return (((c2 * 4 + x2) * 2 + yl2) * 2 + yh2) * 2 + zh2

    own_block = head_block(c, x, yl, yh, z // 8)
    loads[4].wait()
    left, right = head_ref[:, :WIDE], head_ref[:, WIDE:]
    right = jnp.concatenate([right[: OWN // 2], right[OWN // 2 :]], axis=1)
    head_low = jnp.concatenate([left, right, jnp.zeros((1, WIDE), F32)], axis=0).astype(BF16)

    @pl.when(is_source)
    def _():
        hb[own_block] = head_low

    pl.semaphore_wait(barrier, jnp.where(is_source, 15 + 1 + 9, 2 + 1 + 9))

    def head_z(k):
        block = hb.at[own_block]
        return remote(block, block, hz_send.at[k], hz_recv.at[z // 8], to_z(k))

    @pl.when(is_source)
    def _():
        def go(k, carry):
            head_z(k).start()
            return carry

        lax.fori_loop(1, NZ, go, 0)

    def text_copies(src, slot, device, first):
        return [
            remote(s, d, text_send.at[first + i], text_recv.at[first + i], device)
            for i, (s, d) in enumerate(zip(src, (tb.at[slot], tf.at[slot], tl.at[slot])))
        ]

    own_text = (base_hbm, feat_hbm, label_hbm)
    text_y = text_copies(own_text, 2, to_y(2), 0)
    text_c = text_copies(own_text, 1, to_core, 3)
    text_yc = text_copies((tb.at[2], tf.at[2], tl.at[2]), 3, to_core, 6)

    def up(s, k):
        rows = pl.ds(k * PIECE, PIECE)
        src, dst = jnp.maximum(2 * s - 3, 0), 2 * s - 1
        return remote(img.at[src, rows], img.at[dst, rows], up_send.at[s, k], up_recv.at[s, k], to_z(1))

    def dn(s, k):
        rows = pl.ds(k * PIECE, PIECE)
        src, dst = 2 * s - 2, jnp.minimum(2 * s, 15)
        return remote(img.at[src, rows], img.at[dst, rows], dn_send.at[s, k], dn_recv.at[s, k], to_z(NZ - 1))

    for k in range(CHUNKS):
        up(1, k).start()
        dn(1, k).start()
    for copy in text_c:
        copy.start()
    text_y[0].start()
    text_y[2].start()

    def ring(s, chunks=range(CHUNKS)):
        for k in chunks:
            up(s, k).wait_recv()

            @pl.when((s < 7) | (k < CHUNKS // 2))
            def _():
                up(s + 1, k).start()

            dn(s, k).wait_recv()

            @pl.when((s < 7) | (k >= CHUNKS // 2))
            def _():
                dn(s + 1, k).start()

            if s > 1:
                up(s - 1, k).wait_send()
                dn(s - 1, k).wait_send()

    early, late = range(CHUNKS // 2), range(CHUNKS // 2, CHUNKS)

    place = lax.broadcasted_iota(jnp.int32, (1, 64 * PAD), 1)
    block, row = place >> 4, place & 15
    source = ((block >> 3) & 3) + 4 * (((block >> 2) ^ (block >> 5)) & 1) + 8 * (block & 1)
    first_row = (source * 4 + ((block >> 1) & 1) * 2 + (block >> 5)) * OWN
    packed = (row >= OWN) & (row < PAD - 1)
    row_of = lax.broadcasted_iota(jnp.int32, (K, 64 * PAD), 0)
    wanted = jnp.where(row < OWN, first_row + row, jnp.where(packed, first_row + row - OWN, -1))
    pick[0] = (row_of == wanted).astype(F32).astype(BF16)
    def head_y(k):
        blocks = hb.at[pl.ds(head_block(c, x, yl, yh, 0), 2)]
        return remote(blocks, blocks, hy_send.at[k], hy_recv.at[k], to_y(k))

    def head_x(k):
        blocks = hb.at[pl.ds(head_block(c, x, 0, 0, 0), 8)]
        return remote(blocks, blocks, hx_send.at[k], hx_recv.at[k], to_x(k))

    all_mine = hb.at[pl.ds(c * 32, 32)]
    head_c = remote(all_mine, all_mine, hc_send, hc_recv, to_core)

    ring(1, early)
    wanted = jnp.where(packed, first_row + row - OWN // 2, -1)
    pick[1] = (row_of == wanted).astype(F32).astype(BF16)
    place = lax.broadcasted_iota(jnp.int32, (K // 2, 1), 0)
    block = (place * 6554) >> 16
    source = ((block >> 4) & 1) * 2 + ((block >> 2) & 1) + 4 * (block & 3)
    owner = source * 4 + ((block >> 3) & 1) * 2 + c
    wanted = owner * OWN + place - block * OWN
    order[...] = (lax.broadcasted_iota(jnp.int32, (K // 2, K), 1) == wanted).astype(F32).astype(BF16)
    text_y[1].start()
    ring(1, late)
    for zh in range(2):

        @pl.when(z != head_z0 + 8 * zh)
        def _():
            block = hb.at[head_block(c, x, yl, yh, zh)]
            remote(block, block, hz_send.at[0], hz_recv.at[zh], to_z(1)).wait_recv()

    for k in range(1, 4):
        head_y(k).start()
    ring(2)
    for k in range(1, 4):
        head_y(k).wait_recv()
    for k in (2, 1, 3):
        head_x(k).start()
    ring(3)
    ring(4, early)
    for copy in text_y:
        copy.wait_recv()
    for copy in text_yc:
        copy.start()
    ring(4, late)

    for load in loads[1:4]:
        load.wait()
    for copy in text_c + text_yc:
        copy.wait_recv()
    diagonal = lax.broadcasted_iota(jnp.int32, (ROWS, ROWS), 0) == lax.broadcasted_iota(jnp.int32, (ROWS, ROWS), 1)
    for i in range(4):
        column = jnp.sum(jnp.where(diagonal, tl[i].astype(F32), 0.0), axis=1, keepdims=True)
        label_wide[pl.ds(i * ROWS, ROWS)] = jnp.broadcast_to(column, (ROWS, ROWS)).astype(jnp.int32)
    features = tf[...].reshape(4 * ROWS, K)
    whole = jnp.dot(features, pick[0], preferred_element_type=F32)
    spread[0] = jnp.where(row < OWN, whole, 0.0).astype(BF16)
    spread[1] = jnp.where(row < OWN, 0.0, whole).astype(BF16)
    ring(5, early)
    spread[2] = jnp.dot(tf[...].reshape(4 * ROWS, K), pick[1], preferred_element_type=F32).astype(BF16)
    ring(5, late)
    for k in range(1, 4):
        head_x(k).wait_recv()
    head_c.start()
    feat_t[...] = lax.dot_general(order[...], tf[...].reshape(4 * ROWS, K), NT, preferred_element_type=F32).astype(BF16)
    ring(6, early)
    head_c.wait_recv()
    head_all = hb[...].reshape(64 * PAD, WIDE)
    def project(i):
        rows = pl.ds(i * ROWS, ROWS)
        left = jnp.dot(spread[0, rows], head_all, preferred_element_type=F32)
        right = jnp.dot(spread[1, rows], head_all[:, :REST], preferred_element_type=F32)
        right += jnp.dot(spread[2, rows], head_all[:, REST:], preferred_element_type=F32)
        emb = tb[i].astype(F32) + jnp.concatenate([left, right], axis=1)
        inv = lax.rsqrt(jnp.sum(emb * emb, axis=1, keepdims=True) + norm_epsilon)
        exact = emb * inv
        inv_norm[rows] = inv
        text_exact[rows] = exact
        text_unit[rows] = exact.astype(BF16)

    project(0)
    project(1)

    @pl.when(is_source)
    def _():
        def drain_head(k, carry):
            head_z(k).wait_send()
            return carry

        lax.fori_loop(1, NZ, drain_head, 0)

    for copy in text_y + text_c + text_yc:
        copy.wait_send()
    for k in range(1, 4):
        head_y(k).wait_send()
        head_x(k).wait_send()
    ring(6, late)
    project(2)
    project(3)

    lane = lax.broadcasted_iota(jnp.int32, (1, ROWS), 1)

    def columns(z2):
        return ((z2 % NZ) * 4 + yh * 2 + c) * ROWS + lane

    def process(first, blocks, marks, fresh=False):
        images = img[pl.ds(first, blocks)].reshape(blocks * ROWS, D)
        halves = [pl.ds(i * 256, 256) for i in range(2)]
        raws = [lax.dot_general(text_unit[rows], images, NT, preferred_element_type=F32) for rows in halves]
        for rows, raw in zip(halves, raws):
            chance = 0.5 * jnp.tanh((0.5 * logit_scale) * raw + 0.5 * logit_bias) + 0.5
            labels = label_wide[rows]
            match = jnp.concatenate([(labels == columns(z + m + NZ)) for m in marks], axis=1)
            weights = jnp.where(match, chance - 1.0, chance).astype(BF16)
            grad = jnp.dot(weights, images, preferred_element_type=F32)
            if fresh:
                unit_grad[rows] = grad
            else:
                unit_grad[rows] += grad

    process(0, 4, (0, -1, 1, -2), True)
    ring(7, early)
    process(4, 4, (2, -3, 3, -4))
    ring(7, late)
    process(8, 4, (4, -5, 5, -6))
    process(12, 3, (6, -7, 7))
    for k in range(CHUNKS // 2):
        up(8, k).wait_recv()
        dn(8, k + CHUNKS // 2).wait_recv()
    process(15, 1, (8,))

    def drain():
        for k in range(CHUNKS):
            up(7, k).wait_send()
            dn(7, k).wait_send()
        for k in range(CHUNKS // 2):
            up(8, k).wait_send()
            dn(8, k + CHUNKS // 2).wait_send()
        head_c.wait_send()

    def to_other(i):
        rows, there = pl.ds(i * ROWS, ROWS), pl.ds((i ^ 1) * ROWS, ROWS)
        return remote(grad_low.at[rows], grad_in.at[there], gc_send.at[i], gc_recv.at[i], to_core)

    for i in range(4):
        rows = pl.ds(i * ROWS, ROWS)
        exact, grad = text_exact[rows], unit_grad[rows]
        along = jnp.sum(exact * grad, axis=1, keepdims=True)
        grad_low[rows] = ((grad - exact * along) * (logit_scale * inv_norm[rows])).astype(BF16)
        to_other(i).start()

    def x_copy(k):
        src, dst = (x_far_out, x_far_in) if k == 2 else (x_out.at[k // 2], x_in.at[k // 2])
        return remote(src, dst, ga_send.at[0, k], ga_recv.at[0, k], to_x(k))

    def y_copy(k):
        src, dst = (y_far_out, y_far_in) if k == 2 else (y_out.at[k // 2], y_in.at[k // 2])
        return remote(src, dst, gb_send.at[0, k], gb_recv.at[0, k], to_y(k))

    def x_last(k):
        src, dst = (x2_far_out, x2_far_in) if k == 2 else (x2_out.at[k // 2], x2_in.at[k // 2])
        return remote(src, dst, gb_send.at[1, k], gb_recv.at[1, k], to_x(k))

    def y_last(k):
        src, dst = (y2_far_out, y2_far_in) if k == 2 else (y2_out.at[k // 2], y2_in.at[k // 2])
        return remote(src, dst, ga_send.at[1, k], ga_recv.at[1, k], to_y(k))

    def low(parts, rows):
        filler = rows - sum(p.shape[0] for p in parts)
        if filler:
            parts = parts + [jnp.zeros((filler, HALF), F32)]
        return jnp.concatenate(parts, axis=0).astype(BF16)

    for h in range(2):
        partial[h] = jnp.dot(feat_t[pl.ds(h * 160, 160)], grad_low[...], preferred_element_type=F32)
    for i in range(4):
        to_other(i).wait_recv()
    for h in range(2):
        mine = partial[h] + jnp.dot(feat_t[pl.ds(h * 160, 160)], grad_in[...], preferred_element_type=F32)
        for k in range(4):
            for side in range(2):
                piece[2 * h + side, k] = mine[k * 40 : (k + 1) * 40, side * HALF : (side + 1) * HALF]

    def mine_of(dx, dy):
        return piece.at[(x + dx) % 4, (y + dy) % 4]

    top, end = pl.ds(0, FIRST), pl.ds(FIRST, SECOND)
    for k in (1, 3):
        x_out[k // 2] = low([mine_of(k, 0)[top], mine_of(k, 1)[top], mine_of(k, 3)[top], mine_of(k, 2)[...]], 112)
        x_copy(k).start()
    x_far_out[...] = low([mine_of(2, 2)[top]], 32)
    x_copy(2).start()
    for k in (1, 3):
        y_out[k // 2] = low([mine_of(0, k)[end], mine_of(1, k)[end], mine_of(3, k)[end], mine_of(2, k)[...]], 96)
        y_copy(k).start()
    y_far_out[...] = low([mine_of(2, 2)[end]], 16)
    y_copy(2).start()
    drain()

    for k in (1, 3, 2):
        y_copy(k).wait_recv()
    came = y_in[0].astype(F32) + y_in[1].astype(F32)
    x2_far_out[...] = low(
        [mine_of(2, 0)[top] + came[48 : 48 + FIRST], mine_of(2, 0)[end] + came[48 + FIRST : 88] + y_far_in[...].astype(F32)], 48
    )
    x_last(2).start()
    x2_out[0] = (mine_of(1, 0)[end] + came[16:32]).astype(BF16)
    x_last(1).start()
    x2_out[1] = (mine_of(3, 0)[end] + came[32:48]).astype(BF16)
    x_last(3).start()
    second = mine_of(0, 0)[end] + came[:16]

    for k in (1, 3, 2):
        x_copy(k).wait_recv()
    came = x_in[0].astype(F32) + x_in[1].astype(F32)
    y2_far_out[...] = low(
        [mine_of(0, 2)[top] + came[72 : 72 + FIRST] + x_far_in[pl.ds(0, FIRST)].astype(F32), mine_of(0, 2)[end] + came[72 + FIRST :]],
        48,
    )
    y_last(2).start()
    y2_out[0] = low([mine_of(0, 1)[top] + came[FIRST : 2 * FIRST]], 32)
    y_last(1).start()
    y2_out[1] = low([mine_of(0, 3)[top] + came[2 * FIRST : 3 * FIRST]], 32)
    y_last(3).start()
    first = mine_of(0, 0)[top] + came[:FIRST]

    for k in (1, 3, 2):
        x_last(k).wait_recv()
    second += x2_in[0].astype(F32) + x2_in[1].astype(F32)
    for k in (1, 3, 2):
        y_last(k).wait_recv()
    first += y2_in[0, :FIRST].astype(F32) + y2_in[1, :FIRST].astype(F32)
    total = jnp.concatenate([first, second], axis=0)
    total += x2_far_in[:40].astype(F32) + y2_far_in[:40].astype(F32)
    for j in range(4):
        part = total[j * OWN : (j + 1) * OWN]
        thirds = [part[:, i * 128 : (i + 1) * 128] for i in range(3)] + [jnp.zeros((2, 128), F32)]
        z_out[j] = jnp.concatenate(thirds, axis=0).astype(BF16)

    group = 2 * (x // 2) + yl

    def to_z_part(j):
        k = (group + 4 * j - z + NZ) % NZ
        return remote(z_out.at[j], z_in.at[k], gz_send.at[j], gz_recv, to_z(k))

    for j in range(4):

        @pl.when(z != group + 4 * j)
        def _():
            to_z_part(j).start()

    is_owner = (z % 4) == group
    side = x % 2

    def to_share(i):
        rep2 = (rep + i) % 8
        device = (dp, rep2)
        return remote(share.at[side], share.at[side], gs_send.at[i], gs_recv.at[side], device)

    @pl.when(is_owner)
    def _():
        z_in[0] = z_out[z // 4]
        others = z_in.at[pl.ds(1, NZ - 1)]
        remote(others, others, gz_send.at[0], gz_recv, to_z(1)).wait_recv()
        share[side] = jnp.sum(z_in[...].astype(F32), axis=0)
        for i in range(1, 8):
            to_share(i).start()

    for s in range(2):

        @pl.when(jnp.logical_not(is_owner & (side == s)))
        def _():
            remote(share.at[s], share.at[s], gs_send.at[0], gs_recv.at[s], to_x(1)).wait_recv()

    pieces = [share[s, i * OWN : (i + 1) * OWN] for s in range(2) for i in range(3)]
    head_grad_ref[...] = jnp.concatenate(pieces, axis=1) * (1.0 / 8.0)

    for k in range(1, 4):
        x_copy(k).wait_send()
        y_copy(k).wait_send()
        x_last(k).wait_send()
        y_last(k).wait_send()
    for i in range(4):
        to_other(i).wait_send()
    for j in range(4):

        @pl.when(z != group + 4 * j)
        def _():
            to_z_part(j).wait_send()

    @pl.when(is_owner)
    def _():
        for i in range(1, 8):
            to_share(i).wait_send()


def per_device(img_emb, txt_base, txt_feat, head, momentum, positive_image):
    vmem = pl.BlockSpec(memory_space=pltpu.VMEM)
    hbm = pl.BlockSpec(memory_space=pl.ANY)
    dma = pltpu.SemaphoreType.DMA
    texts = 4 * ROWS
    out = jax.ShapeDtypeStruct((OWN, D), F32)
    head_grad = pl.pallas_call(
        kernel,
        out_shape=out,
        in_specs=[hbm] * 5,
        out_specs=vmem,
        scratch_shapes=[
            pltpu.VMEM((ROWS, D), BF16),
            pltpu.VMEM((OWN, D), F32),
            pltpu.VMEM((NZ, ROWS, D), BF16),
            pltpu.VMEM((4, ROWS, D), BF16),
            pltpu.VMEM((4, ROWS, K), BF16),
            pltpu.VMEM((4, 1, ROWS), jnp.int32),
            pltpu.VMEM((64, PAD, WIDE), BF16),
            pltpu.VMEM((2, K, 64 * PAD), BF16),
            pltpu.VMEM((K // 2, K), BF16),
            pltpu.VMEM((3, texts, 64 * PAD), BF16),
            pltpu.VMEM((K // 2, texts), BF16),
            pltpu.VMEM((texts, D), F32),
            pltpu.VMEM((texts, D), BF16),
            pltpu.VMEM((texts, 1), F32),
            pltpu.VMEM((texts, ROWS), jnp.int32),
            pltpu.VMEM((texts, D), F32),
            pltpu.VMEM((texts, D), BF16),
            pltpu.VMEM((texts, D), BF16),
            pltpu.VMEM((2, 160, D), F32),
            pltpu.VMEM((4, 4, 40, HALF), F32),
            pltpu.VMEM((2, 112, HALF), BF16),
            pltpu.VMEM((2, 112, HALF), BF16),
            pltpu.VMEM((32, HALF), BF16),
            pltpu.VMEM((32, HALF), BF16),
            pltpu.VMEM((2, 96, HALF), BF16),
            pltpu.VMEM((2, 96, HALF), BF16),
            pltpu.VMEM((SECOND, HALF), BF16),
            pltpu.VMEM((SECOND, HALF), BF16),
            pltpu.VMEM((2, SECOND, HALF), BF16),
            pltpu.VMEM((2, SECOND, HALF), BF16),
            pltpu.VMEM((48, HALF), BF16),
            pltpu.VMEM((48, HALF), BF16),
            pltpu.VMEM((2, 32, HALF), BF16),
            pltpu.VMEM((2, 32, HALF), BF16),
            pltpu.VMEM((48, HALF), BF16),
            pltpu.VMEM((48, HALF), BF16),
            pltpu.VMEM((4, 32, 128), BF16),
            pltpu.VMEM((NZ, 32, 128), BF16),
            pltpu.VMEM((2, 32, 128), F32),
            dma((5,)),
            dma((9, CHUNKS)),
            dma((9, CHUNKS)),
            dma((9, CHUNKS)),
            dma((9, CHUNKS)),
            dma((9,)),
            dma((9,)),
            dma((NZ,)),
            dma((2,)),
            dma((4,)),
            dma((4,)),
            dma((4,)),
            dma((4,)),
            dma,
            dma,
            dma((4,)),
            dma((4,)),
            dma((2, 4)),
            dma((2, 4)),
            dma((2, 4)),
            dma((2, 4)),
            dma((4,)),
            dma,
            dma((8,)),
            dma((2,)),
        ],
        compiler_params=pltpu.CompilerParams(
            collective_id=0, has_side_effects=True, vmem_limit_bytes=63 * 1024 * 1024
        ),
        cost_estimate=pl.CostEstimate(flops=8_000_000_000, bytes_accessed=2_000_000, transcendentals=1_100_000),
        name="contrastive_step",
    )(img_emb[0], txt_base[0], txt_feat[0], head, positive_image)
    new_momentum = momentum_decay * momentum + (1.0 - momentum_decay) * head_grad
    new_head = head - outer_rate * ((1.0 - blend_weight) * head_grad + blend_weight * new_momentum)
    return (new_head, new_momentum)


def solution(mesh):
    placed = (
        P("replica", "dp", None),
        P("replica", "dp", None),
        P("replica", "dp", None),
        P("dp", None),
        P("dp", None),
        P("replica", "dp"),
    )
    return jax.shard_map(
        per_device,
        mesh=mesh,
        in_specs=placed,
        out_specs=(P("dp", None), P("dp", None)),
        check_vma=False,
    )
```

```python
import functools

import jax
import jax.numpy as jnp
from jax import lax
from jax.experimental import pallas as pl
from jax.experimental.pallas import tpu as pltpu
from jax.sharding import PartitionSpec as P

MESH = pl.DeviceIdType.MESH
F32 = jnp.float32
BF16 = jnp.bfloat16

logit_scale = 10.0
logit_bias = -3.0
norm_epsilon = 1e-06
momentum_decay = 0.9
blend_weight = 0.7
outer_rate = 0.7

NZ = 16
ROWS = 128
D = 768
K = 640
OWN = 10
PAD = 16
WIDE = 512
REST = D - WIDE
FIRST = 24
SECOND = 16
HALF = D // 2
NT = (((1,), (1,)), ((), ()))
CHUNKS = 4
PIECE = ROWS // CHUNKS


def kernel(
    img_hbm,
    base_hbm,
    feat_hbm,
    head_hbm,
    label_hbm,
    head_grad_ref,
    img_raw,
    head_ref,
    img,
    tb,
    tf,
    tl,
    hb,
    pick,
    order,
    spread,
    feat_t,
    text_exact,
    text_unit,
    inv_norm,
    label_wide,
    unit_grad,
    grad_low,
    grad_in,
    partial,
    piece,
    x_out,
    x_in,
    x_far_out,
    x_far_in,
    y_out,
    y_in,
    x2_out,
    x2_in,
    x2_far_out,
    x2_far_in,
    y2_out,
    y2_in,
    y2_far_out,
    y2_far_in,
    z_out,
    z_in,
    share,
    local_sem,
    up_send,
    up_recv,
    dn_send,
    dn_recv,
    text_send,
    text_recv,
    hz_send,
    hz_recv,
    hy_send,
    hy_recv,
    hx_send,
    hx_recv,
    hc_send,
    hc_recv,
    gc_send,
    gc_recv,
    ga_send,
    ga_recv,
    gb_send,
    gb_recv,
    gz_send,
    gz_recv,
    gs_send,
    gs_recv,
):
    dp = lax.axis_index("dp")
    rep = lax.axis_index("replica")
    z, yh, c = dp // 4, (dp // 2) % 2, dp % 2
    yl, x = rep // 4, rep % 4
    y = yl + 2 * yh

    def at(z2, y2, x2, c2):
        return (z2 * 4 + (y2 // 2) * 2 + c2, (y2 % 2) * 4 + x2)

    def to_z(k):
        return at((z + k) % NZ, y, x, c)

    def to_y(k):
        return at(z, (y + k) % 4, x, c)

    def to_x(k):
        return at(z, y, (x + k) % 4, c)

    to_core = at(z, y, x, 1 - c)

    def remote(src, dst, send, recv, device):
        return pltpu.make_async_remote_copy(
            src_ref=src, dst_ref=dst, send_sem=send, recv_sem=recv, device_id=device, device_id_type=MESH
        )

    loads = [
        pltpu.make_async_copy(img_hbm, img_raw, local_sem.at[0]),
        pltpu.make_async_copy(base_hbm, tb.at[0], local_sem.at[1]),
        pltpu.make_async_copy(feat_hbm, tf.at[0], local_sem.at[2]),
        pltpu.make_async_copy(label_hbm, tl.at[0], local_sem.at[3]),
        pltpu.make_async_copy(head_hbm, head_ref, local_sem.at[4]),
    ]
    for load in loads:
        load.start()

    barrier = pltpu.get_barrier_semaphore()

    def greet(device):
        pl.semaphore_signal(barrier, inc=1, device_id=device, device_id_type=MESH)

    head_z0 = (rep + 4 * c) % 8
    is_source = (z % 8) == head_z0
    greet(to_z(1))
    greet(to_z(NZ - 1))
    greet(to_core)
    for k in range(1, 4):
        greet(to_x(k))
        greet(to_y(k))
        greet(at(z, yh * 2 + (1 - yl), (x + k) % 4, c))
    for zh in range(2):
        away = (head_z0 + 8 * zh - z + NZ) % NZ

        @pl.when((away > 1) & (away < NZ - 1))
        def _():
            greet(to_z(away))

    loads[0].wait()
    wide = img_raw[...].astype(F32)
    img[0] = (wide * lax.rsqrt(jnp.sum(wide * wide, axis=1, keepdims=True) + norm_epsilon)).astype(BF16)

    def head_block(c2, x2, yl2, yh2, zh2):
        return (((c2 * 4 + x2) * 2 + yl2) * 2 + yh2) * 2 + zh2

    own_block = head_block(c, x, yl, yh, z // 8)
    loads[4].wait()
    left, right = head_ref[:, :WIDE], head_ref[:, WIDE:]
    right = jnp.concatenate([right[: OWN // 2], right[OWN // 2 :]], axis=1)
    head_low = jnp.concatenate([left, right, jnp.zeros((1, WIDE), F32)], axis=0).astype(BF16)

    @pl.when(is_source)
    def _():
        hb[own_block] = head_low

    pl.semaphore_wait(barrier, jnp.where(is_source, 15 + 1 + 9, 2 + 1 + 9))

    def head_z(k):
        block = hb.at[own_block]
        return remote(block, block, hz_send.at[k], hz_recv.at[z // 8], to_z(k))

    @pl.when(is_source)
    def _():
        def go(k, carry):
            head_z(k).start()
            return carry

        lax.fori_loop(1, NZ, go, 0)

    def text_copies(src, slot, device, first):
        return [
            remote(s, d, text_send.at[first + i], text_recv.at[first + i], device)
            for i, (s, d) in enumerate(zip(src, (tb.at[slot], tf.at[slot], tl.at[slot])))
        ]

    own_text = (base_hbm, feat_hbm, label_hbm)
    text_y = text_copies(own_text, 2, to_y(2), 0)
    text_c = text_copies(own_text, 1, to_core, 3)
    text_yc = text_copies((tb.at[2], tf.at[2], tl.at[2]), 3, to_core, 6)

    def up(s, k):
        rows = pl.ds(k * PIECE, PIECE)
        src, dst = jnp.maximum(2 * s - 3, 0), 2 * s - 1
        return remote(img.at[src, rows], img.at[dst, rows], up_send.at[s, k], up_recv.at[s, k], to_z(1))

    def dn(s, k):
        rows = pl.ds(k * PIECE, PIECE)
        src, dst = 2 * s - 2, jnp.minimum(2 * s, 15)
        return remote(img.at[src, rows], img.at[dst, rows], dn_send.at[s, k], dn_recv.at[s, k], to_z(NZ - 1))

    for k in range(CHUNKS):
        up(1, k).start()
        dn(1, k).start()
    for copy in text_c:
        copy.start()
    text_y[0].start()
    text_y[2].start()

    def ring(s, chunks=range(CHUNKS)):
        for k in chunks:
            up(s, k).wait_recv()

            @pl.when((s < 7) | (k < CHUNKS // 2))
            def _():
                up(s + 1, k).start()

            dn(s, k).wait_recv()

            @pl.when((s < 7) | (k >= CHUNKS // 2))
            def _():
                dn(s + 1, k).start()

            if s > 1:
                up(s - 1, k).wait_send()
                dn(s - 1, k).wait_send()

    early, late = range(CHUNKS // 2), range(CHUNKS // 2, CHUNKS)

    place = lax.broadcasted_iota(jnp.int32, (1, 64 * PAD), 1)
    block, row = place >> 4, place & 15
    source = ((block >> 3) & 3) + 4 * (((block >> 2) ^ (block >> 5)) & 1) + 8 * (block & 1)
    first_row = (source * 4 + ((block >> 1) & 1) * 2 + (block >> 5)) * OWN
    packed = (row >= OWN) & (row < PAD - 1)
    row_of = lax.broadcasted_iota(jnp.int32, (K, 64 * PAD), 0)
    wanted = jnp.where(row < OWN, first_row + row, jnp.where(packed, first_row + row - OWN, -1))
    pick[0] = (row_of == wanted).astype(F32).astype(BF16)
    def head_y(k):
        blocks = hb.at[pl.ds(head_block(c, x, yl, yh, 0), 2)]
        return remote(blocks, blocks, hy_send.at[k], hy_recv.at[k], to_y(k))

    def head_x(k):
        blocks = hb.at[pl.ds(head_block(c, x, 0, 0, 0), 8)]
        return remote(blocks, blocks, hx_send.at[k], hx_recv.at[k], to_x(k))

    all_mine = hb.at[pl.ds(c * 32, 32)]
    head_c = remote(all_mine, all_mine, hc_send, hc_recv, to_core)

    ring(1, early)
    wanted = jnp.where(packed, first_row + row - OWN // 2, -1)
    pick[1] = (row_of == wanted).astype(F32).astype(BF16)
    place = lax.broadcasted_iota(jnp.int32, (K // 2, 1), 0)
    block = (place * 6554) >> 16
    source = ((block >> 4) & 1) * 2 + ((block >> 2) & 1) + 4 * (block & 3)
    owner = source * 4 + ((block >> 3) & 1) * 2 + c
    wanted = owner * OWN + place - block * OWN
    order[...] = (lax.broadcasted_iota(jnp.int32, (K // 2, K), 1) == wanted).astype(F32).astype(BF16)
    text_y[1].start()
    ring(1, late)
    for zh in range(2):

        @pl.when(z != head_z0 + 8 * zh)
        def _():
            block = hb.at[head_block(c, x, yl, yh, zh)]
            remote(block, block, hz_send.at[0], hz_recv.at[zh], to_z(1)).wait_recv()

    for k in range(1, 4):
        head_y(k).start()
    ring(2)
    for k in range(1, 4):
        head_y(k).wait_recv()
    for k in (2, 1, 3):
        head_x(k).start()
    ring(3)
    ring(4, early)
    for copy in text_y:
        copy.wait_recv()
    for copy in text_yc:
        copy.start()
    ring(4, late)

    for load in loads[1:4]:
        load.wait()
    for copy in text_c + text_yc:
        copy.wait_recv()
    diagonal = lax.broadcasted_iota(jnp.int32, (ROWS, ROWS), 0) == lax.broadcasted_iota(jnp.int32, (ROWS, ROWS), 1)
    for i in range(4):
        column = jnp.sum(jnp.where(diagonal, tl[i].astype(F32), 0.0), axis=1, keepdims=True)
        label_wide[pl.ds(i * ROWS, ROWS)] = jnp.broadcast_to(column, (ROWS, ROWS)).astype(jnp.int32)
    features = tf[...].reshape(4 * ROWS, K)
    whole = jnp.dot(features, pick[0], preferred_element_type=F32)
    spread[0] = jnp.where(row < OWN, whole, 0.0).astype(BF16)
    spread[1] = jnp.where(row < OWN, 0.0, whole).astype(BF16)
    ring(5, early)
    spread[2] = jnp.dot(tf[...].reshape(4 * ROWS, K), pick[1], preferred_element_type=F32).astype(BF16)
    ring(5, late)
    for k in range(1, 4):
        head_x(k).wait_recv()
    head_c.start()
    feat_t[...] = lax.dot_general(order[...], tf[...].reshape(4 * ROWS, K), NT, preferred_element_type=F32).astype(BF16)
    ring(6, early)
    head_c.wait_recv()
    head_all = hb[...].reshape(64 * PAD, WIDE)
    def project(i):
        rows = pl.ds(i * ROWS, ROWS)
        left = jnp.dot(spread[0, rows], head_all, preferred_element_type=F32)
        right = jnp.dot(spread[1, rows], head_all[:, :REST], preferred_element_type=F32)
        right += jnp.dot(spread[2, rows], head_all[:, REST:], preferred_element_type=F32)
        emb = tb[i].astype(F32) + jnp.concatenate([left, right], axis=1)
        inv = lax.rsqrt(jnp.sum(emb * emb, axis=1, keepdims=True) + norm_epsilon)
        exact = emb * inv
        inv_norm[rows] = inv
        text_exact[rows] = exact
        text_unit[rows] = exact.astype(BF16)

    project(0)
    project(1)

    @pl.when(is_source)
    def _():
        def drain_head(k, carry):
            head_z(k).wait_send()
            return carry

        lax.fori_loop(1, NZ, drain_head, 0)

    for copy in text_y + text_c + text_yc:
        copy.wait_send()
    for k in range(1, 4):
        head_y(k).wait_send()
        head_x(k).wait_send()
    ring(6, late)
    project(2)
    project(3)

    lane = lax.broadcasted_iota(jnp.int32, (1, ROWS), 1)

    def columns(z2):
        return ((z2 % NZ) * 4 + yh * 2 + c) * ROWS + lane

    def process(first, blocks, marks, fresh=False):
        images = img[pl.ds(first, blocks)].reshape(blocks * ROWS, D)
        halves = [pl.ds(i * 256, 256) for i in range(2)]
        raws = [lax.dot_general(text_unit[rows], images, NT, preferred_element_type=F32) for rows in halves]
        for rows, raw in zip(halves, raws):
            chance = 0.5 * jnp.tanh((0.5 * logit_scale) * raw + 0.5 * logit_bias) + 0.5
            labels = label_wide[rows]
            match = jnp.concatenate([(labels == columns(z + m + NZ)) for m in marks], axis=1)
            weights = jnp.where(match, chance - 1.0, chance).astype(BF16)
            grad = jnp.dot(weights, images, preferred_element_type=F32)
            if fresh:
                unit_grad[rows] = grad
            else:
                unit_grad[rows] += grad

    process(0, 4, (0, -1, 1, -2), True)
    ring(7, early)
    process(4, 4, (2, -3, 3, -4))
    ring(7, late)
    process(8, 4, (4, -5, 5, -6))
    process(12, 3, (6, -7, 7))
    for k in range(CHUNKS // 2):
        up(8, k).wait_recv()
        dn(8, k + CHUNKS // 2).wait_recv()
    process(15, 1, (8,))

    def drain():
        for k in range(CHUNKS):
            up(7, k).wait_send()
            dn(7, k).wait_send()
        for k in range(CHUNKS // 2):
            up(8, k).wait_send()
            dn(8, k + CHUNKS // 2).wait_send()
        head_c.wait_send()

    def to_other(i):
        rows = pl.ds(2 * i, 2)
        return remote(grad_low.at[rows], grad_in.at[rows], gc_send.at[i], gc_recv.at[i], to_core)

    for i in range(4):
        rows = pl.ds(i * ROWS, ROWS)
        exact, grad = text_exact[rows], unit_grad[rows]
        along = jnp.sum(exact * grad, axis=1, keepdims=True)
        grad_low[i] = ((grad - exact * along) * (logit_scale * inv_norm[rows])).astype(BF16)
        if i % 2 == 1:
            to_other(i // 2).start()

    def x_copy(k):
        src, dst = (x_far_out, x_far_in) if k == 2 else (x_out.at[k // 2], x_in.at[k // 2])
        return remote(src, dst, ga_send.at[0, k], ga_recv.at[0, k], to_x(k))

    def y_copy(k):
        return remote(y_out.at[k // 2], y_in.at[k // 2], gb_send.at[0, k], gb_recv.at[0, k], to_y(k))

    def x_last(k):
        src, dst = (x2_far_out, x2_far_in) if k == 2 else (x2_out.at[k // 2], x2_in.at[k // 2])
        return remote(src, dst, gb_send.at[1, k], gb_recv.at[1, k], to_x(k))

    def y_last(k):
        src, dst = (y2_far_out, y2_far_in) if k == 2 else (y2_out.at[k // 2], y2_in.at[k // 2])
        return remote(src, dst, ga_send.at[1, k], ga_recv.at[1, k], to_y(k))

    def low(parts, rows):
        filler = rows - sum(p.shape[0] for p in parts)
        if filler:
            parts = parts + [jnp.zeros((filler, HALF), F32)]
        return jnp.concatenate(parts, axis=0).astype(BF16)

    for h in range(2):
        partial[h] = jnp.dot(feat_t[pl.ds(h * 160, 160)], grad_low[...].reshape(4 * ROWS, D), preferred_element_type=F32)
    for i in range(2):
        to_other(i).wait_recv()
    others_grad = jnp.concatenate([grad_in[i ^ 1] for i in range(4)], axis=0)
    for h in range(2):
        mine = partial[h] + jnp.dot(feat_t[pl.ds(h * 160, 160)], others_grad, preferred_element_type=F32)
        for k in range(4):
            for side in range(2):
                piece[2 * h + side, k] = mine[k * 40 : (k + 1) * 40, side * HALF : (side + 1) * HALF]

    def mine_of(dx, dy):
        return piece.at[(x + dx) % 4, (y + dy) % 4]

    top, end = pl.ds(0, FIRST), pl.ds(FIRST, SECOND)
    for k in (1, 3):
        x_out[k // 2] = low([mine_of(k, 0)[top], mine_of(k, 1)[top], mine_of(k, 3)[top], mine_of(k, 2)[...]], 112)
        x_copy(k).start()
    x_far_out[...] = low([mine_of(2, 2)[...]], 48)
    x_copy(2).start()
    for k in (1, 3):
        y_out[k // 2] = low([mine_of(0, k)[end], mine_of(1, k)[end], mine_of(3, k)[end], mine_of(2, k)[...]], 96)
        y_copy(k).start()
    drain()

    for k in (1, 3):
        y_copy(k).wait_recv()
    came = y_in[0].astype(F32) + y_in[1].astype(F32)
    x2_far_out[...] = low(
        [mine_of(2, 0)[top] + came[48 : 48 + FIRST], mine_of(2, 0)[end] + came[48 + FIRST : 88]], 48
    )
    x_last(2).start()
    x2_out[0] = (mine_of(1, 0)[end] + came[16:32]).astype(BF16)
    x_last(1).start()
    x2_out[1] = (mine_of(3, 0)[end] + came[32:48]).astype(BF16)
    x_last(3).start()
    second = mine_of(0, 0)[end] + came[:16]

    for k in (1, 3, 2):
        x_copy(k).wait_recv()
    came = x_in[0].astype(F32) + x_in[1].astype(F32)
    far_in = x_far_in[...].astype(F32)
    y2_far_out[...] = low([mine_of(0, 2)[...] + came[72:] + far_in[:40]], 48)
    y_last(2).start()
    y2_out[0] = low([mine_of(0, 1)[top] + came[FIRST : 2 * FIRST]], 32)
    y_last(1).start()
    y2_out[1] = low([mine_of(0, 3)[top] + came[2 * FIRST : 3 * FIRST]], 32)
    y_last(3).start()
    first = mine_of(0, 0)[top] + came[:FIRST]

    for k in (1, 3, 2):
        x_last(k).wait_recv()
    second += x2_in[0].astype(F32) + x2_in[1].astype(F32)
    for k in (1, 3, 2):
        y_last(k).wait_recv()
    first += y2_in[0, :FIRST].astype(F32) + y2_in[1, :FIRST].astype(F32)
    total = jnp.concatenate([first, second], axis=0)
    total += x2_far_in[:40].astype(F32) + y2_far_in[:40].astype(F32)
    for j in range(4):
        part = total[j * OWN : (j + 1) * OWN]
        thirds = [part[:, i * 128 : (i + 1) * 128] for i in range(3)] + [jnp.zeros((2, 128), F32)]
        z_out[j] = jnp.concatenate(thirds, axis=0).astype(BF16)

    group = 2 * (x // 2) + yl

    def to_z_part(j):
        k = (group + 4 * j - z + NZ) % NZ
        return remote(z_out.at[j], z_in.at[k], gz_send.at[j], gz_recv, to_z(k))

    for j in range(4):

        @pl.when(z != group + 4 * j)
        def _():
            to_z_part(j).start()

    is_owner = (z % 4) == group
    side = x % 2

    def to_share(i):
        rep2 = (rep + i) % 8
        device = (dp, rep2)
        return remote(share.at[side], share.at[side], gs_send.at[i], gs_recv.at[side], device)

    @pl.when(is_owner)
    def _():
        z_in[0] = z_out[z // 4]
        others = z_in.at[pl.ds(1, NZ - 1)]
        remote(others, others, gz_send.at[0], gz_recv, to_z(1)).wait_recv()
        share[side] = jnp.sum(z_in[...].astype(F32), axis=0)
        for i in range(1, 8):
            to_share(i).start()

    for s in range(2):

        @pl.when(jnp.logical_not(is_owner & (side == s)))
        def _():
            remote(share.at[s], share.at[s], gs_send.at[0], gs_recv.at[s], to_x(1)).wait_recv()

    pieces = [share[s, i * OWN : (i + 1) * OWN] for s in range(2) for i in range(3)]
    head_grad_ref[...] = jnp.concatenate(pieces, axis=1) * (1.0 / 8.0)

    for k in range(1, 4):
        x_copy(k).wait_send()
        if k != 2:
            y_copy(k).wait_send()
        x_last(k).wait_send()
        y_last(k).wait_send()
    for i in range(2):
        to_other(i).wait_send()
    for j in range(4):

        @pl.when(z != group + 4 * j)
        def _():
            to_z_part(j).wait_send()

    @pl.when(is_owner)
    def _():
        for i in range(1, 8):
            to_share(i).wait_send()


def per_device(img_emb, txt_base, txt_feat, head, momentum, positive_image):
    vmem = pl.BlockSpec(memory_space=pltpu.VMEM)
    hbm = pl.BlockSpec(memory_space=pl.ANY)
    dma = pltpu.SemaphoreType.DMA
    texts = 4 * ROWS
    out = jax.ShapeDtypeStruct((OWN, D), F32)
    head_grad = pl.pallas_call(
        kernel,
        out_shape=out,
        in_specs=[hbm] * 5,
        out_specs=vmem,
        scratch_shapes=[
            pltpu.VMEM((ROWS, D), BF16),
            pltpu.VMEM((OWN, D), F32),
            pltpu.VMEM((NZ, ROWS, D), BF16),
            pltpu.VMEM((4, ROWS, D), BF16),
            pltpu.VMEM((4, ROWS, K), BF16),
            pltpu.VMEM((4, 1, ROWS), jnp.int32),
            pltpu.VMEM((64, PAD, WIDE), BF16),
            pltpu.VMEM((2, K, 64 * PAD), BF16),
            pltpu.VMEM((K // 2, K), BF16),
            pltpu.VMEM((3, texts, 64 * PAD), BF16),
            pltpu.VMEM((K // 2, texts), BF16),
            pltpu.VMEM((texts, D), F32),
            pltpu.VMEM((texts, D), BF16),
            pltpu.VMEM((texts, 1), F32),
            pltpu.VMEM((texts, ROWS), jnp.int32),
            pltpu.VMEM((texts, D), F32),
            pltpu.VMEM((4, ROWS, D), BF16),
            pltpu.VMEM((4, ROWS, D), BF16),
            pltpu.VMEM((2, 160, D), F32),
            pltpu.VMEM((4, 4, 40, HALF), F32),
            pltpu.VMEM((2, 112, HALF), BF16),
            pltpu.VMEM((2, 112, HALF), BF16),
            pltpu.VMEM((48, HALF), BF16),
            pltpu.VMEM((48, HALF), BF16),
            pltpu.VMEM((2, 96, HALF), BF16),
            pltpu.VMEM((2, 96, HALF), BF16),
            pltpu.VMEM((2, SECOND, HALF), BF16),
            pltpu.VMEM((2, SECOND, HALF), BF16),
            pltpu.VMEM((48, HALF), BF16),
            pltpu.VMEM((48, HALF), BF16),
            pltpu.VMEM((2, 32, HALF), BF16),
            pltpu.VMEM((2, 32, HALF), BF16),
            pltpu.VMEM((48, HALF), BF16),
            pltpu.VMEM((48, HALF), BF16),
            pltpu.VMEM((4, 32, 128), BF16),
            pltpu.VMEM((NZ, 32, 128), BF16),
            pltpu.VMEM((2, 32, 128), F32),
            dma((5,)),
            dma((9, CHUNKS)),
            dma((9, CHUNKS)),
            dma((9, CHUNKS)),
            dma((9, CHUNKS)),
            dma((9,)),
            dma((9,)),
            dma((NZ,)),
            dma((2,)),
            dma((4,)),
            dma((4,)),
            dma((4,)),
            dma((4,)),
            dma,
            dma,
            dma((4,)),
            dma((4,)),
            dma((2, 4)),
            dma((2, 4)),
            dma((2, 4)),
            dma((2, 4)),
            dma((4,)),
            dma,
            dma((8,)),
            dma((2,)),
        ],
        compiler_params=pltpu.CompilerParams(
            collective_id=0, has_side_effects=True, vmem_limit_bytes=63 * 1024 * 1024
        ),
        cost_estimate=pl.CostEstimate(flops=8_000_000_000, bytes_accessed=2_000_000, transcendentals=1_100_000),
        name="contrastive_step",
    )(img_emb[0], txt_base[0], txt_feat[0], head, positive_image)
    new_momentum = momentum_decay * momentum + (1.0 - momentum_decay) * head_grad
    new_head = head - outer_rate * ((1.0 - blend_weight) * head_grad + blend_weight * new_momentum)
    return (new_head, new_momentum)


def solution(mesh):
    placed = (
        P("replica", "dp", None),
        P("replica", "dp", None),
        P("replica", "dp", None),
        P("dp", None),
        P("dp", None),
        P("replica", "dp"),
    )
    return jax.shard_map(
        per_device,
        mesh=mesh,
        in_specs=placed,
        out_specs=(P("dp", None), P("dp", None)),
        check_vma=False,
    )
```

```python
import functools

import jax
import jax.numpy as jnp
from jax import lax
from jax.experimental import pallas as pl
from jax.experimental.pallas import tpu as pltpu
from jax.sharding import PartitionSpec as P

MESH = pl.DeviceIdType.MESH
F32 = jnp.float32
BF16 = jnp.bfloat16

logit_scale = 10.0
logit_bias = -3.0
norm_epsilon = 1e-06
momentum_decay = 0.9
blend_weight = 0.7
outer_rate = 0.7

NZ = 16
ROWS = 128
D = 768
K = 640
OWN = 10
PAD = 16
WIDE = 512
REST = D - WIDE
FIRST = 24
SECOND = 16
HALF = D // 2
NT = (((1,), (1,)), ((), ()))
CHUNKS = 4
PIECE = ROWS // CHUNKS


def kernel(
    img_hbm,
    base_hbm,
    feat_hbm,
    head_hbm,
    label_hbm,
    head_grad_ref,
    img_raw,
    head_ref,
    img,
    tb,
    tf,
    tl,
    hb,
    pick,
    order,
    spread,
    feat_t,
    text_exact,
    text_unit,
    inv_norm,
    label_wide,
    unit_grad,
    grad_low,
    grad_in,
    partial,
    piece,
    x_out,
    x_in,
    x_far_out,
    x_far_in,
    y_out,
    y_in,
    y_far_out,
    y_far_in,
    x2_out,
    x2_in,
    x2_far_out,
    x2_far_in,
    y2_out,
    y2_in,
    y2_far_out,
    y2_far_in,
    z_out,
    z_in,
    share,
    local_sem,
    up_send,
    up_recv,
    dn_send,
    dn_recv,
    text_send,
    text_recv,
    hz_send,
    hz_recv,
    hy_send,
    hy_recv,
    hx_send,
    hx_recv,
    hc_send,
    hc_recv,
    gc_send,
    gc_recv,
    ga_send,
    ga_recv,
    gb_send,
    gb_recv,
    gz_send,
    gz_recv,
    gs_send,
    gs_recv,
):
    dp = lax.axis_index("dp")
    rep = lax.axis_index("replica")
    z, yh, c = dp // 4, (dp // 2) % 2, dp % 2
    yl, x = rep // 4, rep % 4
    y = yl + 2 * yh

    def at(z2, y2, x2, c2):
        return (z2 * 4 + (y2 // 2) * 2 + c2, (y2 % 2) * 4 + x2)

    def to_z(k):
        return at((z + k) % NZ, y, x, c)

    def to_y(k):
        return at(z, (y + k) % 4, x, c)

    def to_x(k):
        return at(z, y, (x + k) % 4, c)

    to_core = at(z, y, x, 1 - c)

    def remote(src, dst, send, recv, device):
        return pltpu.make_async_remote_copy(
            src_ref=src, dst_ref=dst, send_sem=send, recv_sem=recv, device_id=device, device_id_type=MESH
        )

    loads = [
        pltpu.make_async_copy(img_hbm, img_raw, local_sem.at[0]),
        pltpu.make_async_copy(base_hbm, tb.at[0], local_sem.at[1]),
        pltpu.make_async_copy(feat_hbm, tf.at[0], local_sem.at[2]),
        pltpu.make_async_copy(label_hbm, tl.at[0], local_sem.at[3]),
        pltpu.make_async_copy(head_hbm, head_ref, local_sem.at[4]),
    ]
    for load in loads:
        load.start()

    barrier = pltpu.get_barrier_semaphore()

    def greet(device):
        pl.semaphore_signal(barrier, inc=1, device_id=device, device_id_type=MESH)

    head_z0 = (rep + 4 * c) % 8
    is_source = (z % 8) == head_z0
    greet(to_z(1))
    greet(to_z(NZ - 1))
    greet(to_core)
    for k in range(1, 4):
        greet(to_x(k))
        greet(to_y(k))
        greet(at(z, yh * 2 + (1 - yl), (x + k) % 4, c))
    for zh in range(2):
        away = (head_z0 + 8 * zh - z + NZ) % NZ

        @pl.when((away > 1) & (away < NZ - 1))
        def _():
            greet(to_z(away))

    loads[0].wait()
    wide = img_raw[...].astype(F32)
    img[0] = (wide * lax.rsqrt(jnp.sum(wide * wide, axis=1, keepdims=True) + norm_epsilon)).astype(BF16)

    def head_block(c2, x2, yl2, yh2, zh2):
        return (((c2 * 4 + x2) * 2 + yl2) * 2 + yh2) * 2 + zh2

    own_block = head_block(c, x, yl, yh, z // 8)
    loads[4].wait()
    left, right = head_ref[:, :WIDE], head_ref[:, WIDE:]
    right = jnp.concatenate([right[: OWN // 2], right[OWN // 2 :]], axis=1)
    head_low = jnp.concatenate([left, right, jnp.zeros((1, WIDE), F32)], axis=0).astype(BF16)

    @pl.when(is_source)
    def _():
        hb[own_block] = head_low

    pl.semaphore_wait(barrier, jnp.where(is_source, 15 + 1 + 9, 2 + 1 + 9))

    def head_z(k):
        block = hb.at[own_block]
        return remote(block, block, hz_send.at[k], hz_recv.at[z // 8], to_z(k))

    @pl.when(is_source)
    def _():
        def go(k, carry):
            head_z(k).start()
            return carry

        lax.fori_loop(1, NZ, go, 0)

    def text_copies(src, slot, device, first):
        return [
            remote(s, d, text_send.at[first + i], text_recv.at[first + i], device)
            for i, (s, d) in enumerate(zip(src, (tb.at[slot], tf.at[slot], tl.at[slot])))
        ]

    own_text = (base_hbm, feat_hbm, label_hbm)
    text_y = text_copies(own_text, 2, to_y(2), 0)
    text_c = text_copies(own_text, 1, to_core, 3)
    text_yc = text_copies((tb.at[2], tf.at[2], tl.at[2]), 3, to_core, 6)

    def up(s, k):
        rows = pl.ds(k * PIECE, PIECE)
        src, dst = jnp.maximum(2 * s - 3, 0), 2 * s - 1
        return remote(img.at[src, rows], img.at[dst, rows], up_send.at[s, k], up_recv.at[s, k], to_z(1))

    def dn(s, k):
        rows = pl.ds(k * PIECE, PIECE)
        src, dst = 2 * s - 2, jnp.minimum(2 * s, 15)
        return remote(img.at[src, rows], img.at[dst, rows], dn_send.at[s, k], dn_recv.at[s, k], to_z(NZ - 1))

    for k in range(CHUNKS):
        up(1, k).start()
        dn(1, k).start()
    for copy in text_c:
        copy.start()
    text_y[0].start()
    text_y[2].start()

    def ring(s, chunks=range(CHUNKS)):
        for k in chunks:
            up(s, k).wait_recv()

            @pl.when((s < 7) | (k < CHUNKS // 2))
            def _():
                up(s + 1, k).start()

            dn(s, k).wait_recv()

            @pl.when((s < 7) | (k >= CHUNKS // 2))
            def _():
                dn(s + 1, k).start()

            if s > 1:
                up(s - 1, k).wait_send()
                dn(s - 1, k).wait_send()

    early, late = range(CHUNKS // 2), range(CHUNKS // 2, CHUNKS)

    place = lax.broadcasted_iota(jnp.int32, (1, 64 * PAD), 1)
    block, row = place >> 4, place & 15
    source = ((block >> 3) & 3) + 4 * (((block >> 2) ^ (block >> 5)) & 1) + 8 * (block & 1)
    first_row = (source * 4 + ((block >> 1) & 1) * 2 + (block >> 5)) * OWN
    packed = (row >= OWN) & (row < PAD - 1)
    row_of = lax.broadcasted_iota(jnp.int32, (K, 64 * PAD), 0)
    wanted = jnp.where(row < OWN, first_row + row, jnp.where(packed, first_row + row - OWN, -1))
    pick[0] = (row_of == wanted).astype(F32).astype(BF16)
    def head_y(k):
        blocks = hb.at[pl.ds(head_block(c, x, yl, yh, 0), 2)]
        return remote(blocks, blocks, hy_send.at[k], hy_recv.at[k], to_y(k))

    def head_x(k):
        blocks = hb.at[pl.ds(head_block(c, x, 0, 0, 0), 8)]
        return remote(blocks, blocks, hx_send.at[k], hx_recv.at[k], to_x(k))

    all_mine = hb.at[pl.ds(c * 32, 32)]
    head_c = remote(all_mine, all_mine, hc_send, hc_recv, to_core)

    ring(1, early)
    wanted = jnp.where(packed, first_row + row - OWN // 2, -1)
    pick[1] = (row_of == wanted).astype(F32).astype(BF16)
    place = lax.broadcasted_iota(jnp.int32, (K // 2, 1), 0)
    block = (place * 6554) >> 16
    source = ((block >> 4) & 1) * 2 + ((block >> 2) & 1) + 4 * (block & 3)
    owner = source * 4 + ((block >> 3) & 1) * 2 + c
    wanted = owner * OWN + place - block * OWN
    order[...] = (lax.broadcasted_iota(jnp.int32, (K // 2, K), 1) == wanted).astype(F32).astype(BF16)
    text_y[1].start()
    ring(1, late)
    for zh in range(2):

        @pl.when(z != head_z0 + 8 * zh)
        def _():
            block = hb.at[head_block(c, x, yl, yh, zh)]
            remote(block, block, hz_send.at[0], hz_recv.at[zh], to_z(1)).wait_recv()

    for k in range(1, 4):
        head_y(k).start()
    ring(2)
    for k in range(1, 4):
        head_y(k).wait_recv()
    for k in (2, 1, 3):
        head_x(k).start()
    ring(3)
    ring(4, early)
    for copy in text_y:
        copy.wait_recv()
    for copy in text_yc:
        copy.start()
    ring(4, late)

    for load in loads[1:4]:
        load.wait()
    for copy in text_c + text_yc:
        copy.wait_recv()
    diagonal = lax.broadcasted_iota(jnp.int32, (ROWS, ROWS), 0) == lax.broadcasted_iota(jnp.int32, (ROWS, ROWS), 1)
    for i in range(4):
        column = jnp.sum(jnp.where(diagonal, tl[i].astype(F32), 0.0), axis=1, keepdims=True)
        label_wide[pl.ds(i * ROWS, ROWS)] = jnp.broadcast_to(column, (ROWS, ROWS)).astype(jnp.int32)
    features = tf[...].reshape(4 * ROWS, K)
    whole = jnp.dot(features, pick[0], preferred_element_type=F32)
    spread[0] = jnp.where(row < OWN, whole, 0.0).astype(BF16)
    spread[1] = jnp.where(row < OWN, 0.0, whole).astype(BF16)
    ring(5, early)
    spread[2] = jnp.dot(tf[...].reshape(4 * ROWS, K), pick[1], preferred_element_type=F32).astype(BF16)
    ring(5, late)
    for k in range(1, 4):
        head_x(k).wait_recv()
    head_c.start()
    feat_t[...] = lax.dot_general(order[...], tf[...].reshape(4 * ROWS, K), NT, preferred_element_type=F32).astype(BF16)
    ring(6, early)
    head_c.wait_recv()
    head_all = hb[...].reshape(64 * PAD, WIDE)
    def project(i):
        rows = pl.ds(i * ROWS, ROWS)
        left = jnp.dot(spread[0, rows], head_all, preferred_element_type=F32)
        right = jnp.dot(spread[1, rows], head_all[:, :REST], preferred_element_type=F32)
        right += jnp.dot(spread[2, rows], head_all[:, REST:], preferred_element_type=F32)
        emb = tb[i].astype(F32) + jnp.concatenate([left, right], axis=1)
        inv = lax.rsqrt(jnp.sum(emb * emb, axis=1, keepdims=True) + norm_epsilon)
        exact = emb * inv
        inv_norm[rows] = inv
        text_exact[rows] = exact
        text_unit[rows] = exact.astype(BF16)

    project(0)
    project(1)

    @pl.when(is_source)
    def _():
        def drain_head(k, carry):
            head_z(k).wait_send()
            return carry

        lax.fori_loop(1, NZ, drain_head, 0)

    for copy in text_y + text_c + text_yc:
        copy.wait_send()
    for k in range(1, 4):
        head_y(k).wait_send()
        head_x(k).wait_send()
    ring(6, late)
    project(2)
    project(3)

    lane = lax.broadcasted_iota(jnp.int32, (1, ROWS), 1)

    def columns(z2):
        return ((z2 % NZ) * 4 + yh * 2 + c) * ROWS + lane

    def process(first, blocks, marks, fresh=False):
        images = img[pl.ds(first, blocks)].reshape(blocks * ROWS, D)
        halves = [pl.ds(i * 256, 256) for i in range(2)]
        raws = [lax.dot_general(text_unit[rows], images, NT, preferred_element_type=F32) for rows in halves]
        for rows, raw in zip(halves, raws):
            chance = 0.5 * jnp.tanh((0.5 * logit_scale) * raw + 0.5 * logit_bias) + 0.5
            labels = label_wide[rows]
            match = jnp.concatenate([(labels == columns(z + m + NZ)) for m in marks], axis=1)
            weights = jnp.where(match, chance - 1.0, chance).astype(BF16)
            grad = jnp.dot(weights, images, preferred_element_type=F32)
            if fresh:
                unit_grad[rows] = grad
            else:
                unit_grad[rows] += grad

    process(0, 4, (0, -1, 1, -2), True)
    ring(7, early)
    process(4, 4, (2, -3, 3, -4))
    ring(7, late)
    process(8, 7, (4, -5, 5, -6, 6, -7, 7))
    for k in range(CHUNKS // 2):
        up(8, k).wait_recv()
        dn(8, k + CHUNKS // 2).wait_recv()
    process(15, 1, (8,))

    def drain():
        for k in range(CHUNKS):
            up(7, k).wait_send()
            dn(7, k).wait_send()
        for k in range(CHUNKS // 2):
            up(8, k).wait_send()
            dn(8, k + CHUNKS // 2).wait_send()
        head_c.wait_send()

    def to_other(i):
        rows, there = pl.ds(i * ROWS, ROWS), pl.ds((i ^ 1) * ROWS, ROWS)
        return remote(grad_low.at[rows], grad_in.at[there], gc_send.at[i], gc_recv.at[i], to_core)

    for i in range(4):
        rows = pl.ds(i * ROWS, ROWS)
        exact, grad = text_exact[rows], unit_grad[rows]
        along = jnp.sum(exact * grad, axis=1, keepdims=True)
        grad_low[rows] = ((grad - exact * along) * (logit_scale * inv_norm[rows])).astype(BF16)
        to_other(i).start()

    def x_copy(k):
        src, dst = (x_far_out, x_far_in) if k == 2 else (x_out.at[k // 2], x_in.at[k // 2])
        return remote(src, dst, ga_send.at[0, k], ga_recv.at[0, k], to_x(k))

    def y_copy(k):
        src, dst = (y_far_out, y_far_in) if k == 2 else (y_out.at[k // 2], y_in.at[k // 2])
        return remote(src, dst, gb_send.at[0, k], gb_recv.at[0, k], to_y(k))

    def x_last(k):
        src, dst = (x2_far_out, x2_far_in) if k == 2 else (x2_out.at[k // 2], x2_in.at[k // 2])
        return remote(src, dst, gb_send.at[1, k], gb_recv.at[1, k], to_x(k))

    def y_last(k):
        src, dst = (y2_far_out, y2_far_in) if k == 2 else (y2_out.at[k // 2], y2_in.at[k // 2])
        return remote(src, dst, ga_send.at[1, k], ga_recv.at[1, k], to_y(k))

    def low(parts, rows):
        filler = rows - sum(p.shape[0] for p in parts)
        if filler:
            parts = parts + [jnp.zeros((filler, HALF), F32)]
        return jnp.concatenate(parts, axis=0).astype(BF16)

    for h in range(2):
        partial[h] = jnp.dot(feat_t[pl.ds(h * 160, 160)], grad_low[...], preferred_element_type=F32)
    for i in range(4):
        to_other(i).wait_recv()
    for h in range(2):
        mine = partial[h] + jnp.dot(feat_t[pl.ds(h * 160, 160)], grad_in[...], preferred_element_type=F32)
        for k in range(4):
            for side in range(2):
                piece[2 * h + side, k] = mine[k * 40 : (k + 1) * 40, side * HALF : (side + 1) * HALF]

    def mine_of(dx, dy):
        return piece.at[(x + dx) % 4, (y + dy) % 4]

    top, end = pl.ds(0, FIRST), pl.ds(FIRST, SECOND)
    for k in (1, 3):
        x_out[k // 2] = low([mine_of(k, 0)[top], mine_of(k, 1)[top], mine_of(k, 3)[top], mine_of(k, 2)[...]], 112)
        x_copy(k).start()
    x_far_out[...] = low([mine_of(2, 2)[top]], 32)
    x_copy(2).start()
    for k in (1, 3):
        y_out[k // 2] = low([mine_of(0, k)[end], mine_of(1, k)[end], mine_of(3, k)[end], mine_of(2, k)[...]], 96)
        y_copy(k).start()
    y_far_out[...] = low([mine_of(2, 2)[end]], 16)
    y_copy(2).start()
    drain()

    for k in (1, 3, 2):
        y_copy(k).wait_recv()
    came = y_in[0].astype(F32) + y_in[1].astype(F32)
    x2_far_out[...] = low(
        [mine_of(2, 0)[top] + came[48 : 48 + FIRST], mine_of(2, 0)[end] + came[48 + FIRST : 88] + y_far_in[...].astype(F32)], 48
    )
    x_last(2).start()
    x2_out[0] = (mine_of(1, 0)[end] + came[16:32]).astype(BF16)
    x_last(1).start()
    x2_out[1] = (mine_of(3, 0)[end] + came[32:48]).astype(BF16)
    x_last(3).start()
    second = mine_of(0, 0)[end] + came[:16]

    for k in (1, 3, 2):
        x_copy(k).wait_recv()
    came = x_in[0].astype(F32) + x_in[1].astype(F32)
    y2_far_out[...] = low(
        [mine_of(0, 2)[top] + came[72 : 72 + FIRST] + x_far_in[pl.ds(0, FIRST)].astype(F32), mine_of(0, 2)[end] + came[72 + FIRST :]],
        48,
    )
    y_last(2).start()
    y2_out[0] = low([mine_of(0, 1)[top] + came[FIRST : 2 * FIRST]], 32)
    y_last(1).start()
    y2_out[1] = low([mine_of(0, 3)[top] + came[2 * FIRST : 3 * FIRST]], 32)
    y_last(3).start()
    first = mine_of(0, 0)[top] + came[:FIRST]

    for k in (1, 3, 2):
        x_last(k).wait_recv()
    second += x2_in[0].astype(F32) + x2_in[1].astype(F32)
    for k in (1, 3, 2):
        y_last(k).wait_recv()
    first += y2_in[0, :FIRST].astype(F32) + y2_in[1, :FIRST].astype(F32)
    total = jnp.concatenate([first, second], axis=0)
    total += x2_far_in[:40].astype(F32) + y2_far_in[:40].astype(F32)
    for j in range(4):
        part = total[j * OWN : (j + 1) * OWN]
        thirds = [part[:, i * 128 : (i + 1) * 128] for i in range(3)] + [jnp.zeros((2, 128), F32)]
        z_out[j] = jnp.concatenate(thirds, axis=0).astype(BF16)

    group = 2 * (x // 2) + yl

    def to_z_part(j):
        k = (group + 4 * j - z + NZ) % NZ
        return remote(z_out.at[j], z_in.at[k], gz_send.at[j], gz_recv, to_z(k))

    for j in range(4):

        @pl.when(z != group + 4 * j)
        def _():
            to_z_part(j).start()

    is_owner = (z % 4) == group
    side = x % 2

    def to_share(i):
        rep2 = (rep + i) % 8
        device = (dp, rep2)
        return remote(share.at[side], share.at[side], gs_send.at[i], gs_recv.at[side], device)

    @pl.when(is_owner)
    def _():
        z_in[0] = z_out[z // 4]
        others = z_in.at[pl.ds(1, NZ - 1)]
        remote(others, others, gz_send.at[0], gz_recv, to_z(1)).wait_recv()
        share[side] = jnp.sum(z_in[...].astype(F32), axis=0)
        for i in range(1, 8):
            to_share(i).start()

    for s in range(2):

        @pl.when(jnp.logical_not(is_owner & (side == s)))
        def _():
            remote(share.at[s], share.at[s], gs_send.at[0], gs_recv.at[s], to_x(1)).wait_recv()

    pieces = [share[s, i * OWN : (i + 1) * OWN] for s in range(2) for i in range(3)]
    head_grad_ref[...] = jnp.concatenate(pieces, axis=1) * (1.0 / 8.0)

    for k in range(1, 4):
        x_copy(k).wait_send()
        y_copy(k).wait_send()
        x_last(k).wait_send()
        y_last(k).wait_send()
    for i in range(4):
        to_other(i).wait_send()
    for j in range(4):

        @pl.when(z != group + 4 * j)
        def _():
            to_z_part(j).wait_send()

    @pl.when(is_owner)
    def _():
        for i in range(1, 8):
            to_share(i).wait_send()


def per_device(img_emb, txt_base, txt_feat, head, momentum, positive_image):
    vmem = pl.BlockSpec(memory_space=pltpu.VMEM)
    hbm = pl.BlockSpec(memory_space=pl.ANY)
    dma = pltpu.SemaphoreType.DMA
    texts = 4 * ROWS
    out = jax.ShapeDtypeStruct((OWN, D), F32)
    head_grad = pl.pallas_call(
        kernel,
        out_shape=out,
        in_specs=[hbm] * 5,
        out_specs=vmem,
        scratch_shapes=[
            pltpu.VMEM((ROWS, D), BF16),
            pltpu.VMEM((OWN, D), F32),
            pltpu.VMEM((NZ, ROWS, D), BF16),
            pltpu.VMEM((4, ROWS, D), BF16),
            pltpu.VMEM((4, ROWS, K), BF16),
            pltpu.VMEM((4, 1, ROWS), jnp.int32),
            pltpu.VMEM((64, PAD, WIDE), BF16),
            pltpu.VMEM((2, K, 64 * PAD), BF16),
            pltpu.VMEM((K // 2, K), BF16),
            pltpu.VMEM((3, texts, 64 * PAD), BF16),
            pltpu.VMEM((K // 2, texts), BF16),
            pltpu.VMEM((texts, D), F32),
            pltpu.VMEM((texts, D), BF16),
            pltpu.VMEM((texts, 1), F32),
            pltpu.VMEM((texts, ROWS), jnp.int32),
            pltpu.VMEM((texts, D), F32),
            pltpu.VMEM((texts, D), BF16),
            pltpu.VMEM((texts, D), BF16),
            pltpu.VMEM((2, 160, D), F32),
            pltpu.VMEM((4, 4, 40, HALF), F32),
            pltpu.VMEM((2, 112, HALF), BF16),
            pltpu.VMEM((2, 112, HALF), BF16),
            pltpu.VMEM((32, HALF), BF16),
            pltpu.VMEM((32, HALF), BF16),
            pltpu.VMEM((2, 96, HALF), BF16),
            pltpu.VMEM((2, 96, HALF), BF16),
            pltpu.VMEM((SECOND, HALF), BF16),
            pltpu.VMEM((SECOND, HALF), BF16),
            pltpu.VMEM((2, SECOND, HALF), BF16),
            pltpu.VMEM((2, SECOND, HALF), BF16),
            pltpu.VMEM((48, HALF), BF16),
            pltpu.VMEM((48, HALF), BF16),
            pltpu.VMEM((2, 32, HALF), BF16),
            pltpu.VMEM((2, 32, HALF), BF16),
            pltpu.VMEM((48, HALF), BF16),
            pltpu.VMEM((48, HALF), BF16),
            pltpu.VMEM((4, 32, 128), BF16),
            pltpu.VMEM((NZ, 32, 128), BF16),
            pltpu.VMEM((2, 32, 128), F32),
            dma((5,)),
            dma((9, CHUNKS)),
            dma((9, CHUNKS)),
            dma((9, CHUNKS)),
            dma((9, CHUNKS)),
            dma((9,)),
            dma((9,)),
            dma((NZ,)),
            dma((2,)),
            dma((4,)),
            dma((4,)),
            dma((4,)),
            dma((4,)),
            dma,
            dma,
            dma((4,)),
            dma((4,)),
            dma((2, 4)),
            dma((2, 4)),
            dma((2, 4)),
            dma((2, 4)),
            dma((4,)),
            dma,
            dma((8,)),
            dma((2,)),
        ],
        compiler_params=pltpu.CompilerParams(
            collective_id=0, has_side_effects=True, vmem_limit_bytes=63 * 1024 * 1024
        ),
        cost_estimate=pl.CostEstimate(flops=8_000_000_000, bytes_accessed=2_000_000, transcendentals=1_100_000),
        name="contrastive_step",
    )(img_emb[0], txt_base[0], txt_feat[0], head, positive_image)
    new_momentum = momentum_decay * momentum + (1.0 - momentum_decay) * head_grad
    new_head = head - outer_rate * ((1.0 - blend_weight) * head_grad + blend_weight * new_momentum)
    return (new_head, new_momentum)


def solution(mesh):
    placed = (
        P("replica", "dp", None),
        P("replica", "dp", None),
        P("replica", "dp", None),
        P("dp", None),
        P("dp", None),
        P("replica", "dp"),
    )
    return jax.shard_map(
        per_device,
        mesh=mesh,
        in_specs=placed,
        out_specs=(P("dp", None), P("dp", None)),
        check_vma=False,
    )
```
